32 devices in a mesh: rows: 2 (over core), seq: 16 (over z, y, x).
Axes of the slice: x: 2, y: 2, z: 4, core: 2. Of those that a mesh axis runs over, the one named last changes fastest.
Arguments:
- tokens: bfloat16 [2, 2048, 2048], P('rows', 'seq'), may hold values from -6 to 6
- out_grad: bfloat16 [2, 2048, 2048], P('rows', 'seq'), may hold values from -6 to 6
- doc_lengths: int32 [2, 2], P('rows'), may hold values from 1 to 1536, 2048 in all within a row
- norm_attn: bfloat16 [2048], P(('rows', 'seq')), may hold values from 0.099609375 to 1.8984375
- w_qdown: bfloat16 [2048, 1024], P(('rows', 'seq')), may hold values from -0.125 to 0.125
- norm_query: bfloat16 [1024], P(('rows', 'seq')), may hold values from 0.099609375 to 1.8984375
- w_qup: bfloat16 [1024, 4096], P(('rows', 'seq')), may hold values from -0.1875 to 0.1875
- w_key: bfloat16 [2048, 256], P(('rows', 'seq')), may hold values from -0.125 to 0.125
- w_value: bfloat16 [2048, 256], P(('rows', 'seq')), may hold values from -0.125 to 0.125
- w_out: bfloat16 [4096, 2048], P(None, ('rows', 'seq')), may hold values from -0.375 to 0.375
- norm_ffn: bfloat16 [2048], P(('rows', 'seq')), may hold values from 0.099609375 to 1.8984375
- w_gate: bfloat16 [2048, 5632], P('rows', 'seq'), may hold values from -0.125 to 0.125
- w_up: bfloat16 [2048, 5632], P('rows', 'seq'), may hold values from -0.125 to 0.125
- w_down: bfloat16 [5632, 2048], P('seq', 'rows'), may hold values from -0.078125 to 0.078125
Outputs:
- output: bfloat16 [2, 2048, 2048], P('rows', 'seq')
- grad_tokens: bfloat16 [2, 2048, 2048], P('rows', 'seq')
- grad_norm_attn: float32 [2048], P(('rows', 'seq'))
- grad_w_qdown: float32 [2048, 1024], P(('rows', 'seq'))
- grad_norm_query: float32 [1024], P(('rows', 'seq'))
- grad_w_qup: float32 [1024, 4096], P(('rows', 'seq'))
- grad_w_key: float32 [2048, 256], P(('rows', 'seq'))
- grad_w_value: float32 [2048, 256], P(('rows', 'seq'))
- grad_w_out: float32 [4096, 2048], P(None, ('rows', 'seq'))
- grad_norm_ffn: float32 [2048], P(('rows', 'seq'))
- grad_w_gate: float32 [2048, 5632], P('rows', 'seq')
- grad_w_up: float32 [2048, 5632], P('rows', 'seq')
- grad_w_down: float32 [5632, 2048], P('seq', 'rows')
The draws below stay inside these ranges and needn't reach their ends.
Inputs may be any that keep to these rules, and one draw needn't show every extreme that they name: `doc_lengths`: in each row the 2 document lengths add up to 2048; the longest document of every row has at most 1536 tokens.
All inputs are finite; a program needn't handle non-finite values.
Results may differ from the reference program's by a relative error of at most 0.02.
Values may be sent and summed in bfloat16 or wider, within the bound.
No kernel may reach another device: no remote copies, remote signals or barrier semaphores. Data moves between devices by JAX's collectives and lax.ppermute only.
A program may use at most 512 MiB of HBM per device.

```python
import math
import jax
import jax.numpy as jnp
import numpy as np
from jax import lax

D = 2048
QL = 1024
HEADS = 16
HD = 256
FF = 5632
TOK_DEV = 128
HQ = 4096
ROWS = 2
LEN = 2048
NDOC = 2
DOCMAX = 1536


def shard_levels(own_key, dims, split, low, top_value):
    gain = 1.0
    for position, shards_of in split:
        draws = jax.random.uniform(jax.random.fold_in(jax.random.fold_in(own_key, 6), position), (shards_of,), jnp.float32, low / len(split), top_value / len(split))
        gain = gain * jnp.repeat(jnp.exp(draws), dims[position] // shards_of).reshape((-1,) + (1,) * (len(dims) - 1 - position))
    return gain


def profile(amount, total, reach, lean):
    weights = [(1 << 20) // math.isqrt(standing ** lean) + 1 for standing in range(2, amount + 1)]
    surplus, holding = total - reach - (amount - 1), [1] * (amount - 1)
    while surplus > 0:
        candidates = [i for i in range(amount - 1) if holding[i] < reach]
        mass, left = sum([weights[i] for i in candidates]), surplus
        for i in candidates:
            extra = min(reach - holding[i], max(1, left * weights[i] // mass), surplus)
            holding[i] = holding[i] + extra
            surplus = surplus - extra
    return np.array([reach] + holding)


def ragged_sizes(own_key, count, total, most, slope):
    if count == 2:
        one = jax.random.randint(own_key, (), max(1, total - most), min(most, total - 1) + 1)
        return jnp.stack([one, total - one])
    sizes = jnp.asarray(profile(count, total, most, slope), jnp.int32)
    couples = (count - 1) // 2
    source_of, sink = sizes[1:1 + 2 * couples:2], sizes[2:2 + 2 * couples:2]
    room = jnp.minimum(source_of - 1, most - sink)
    moved = jax.random.randint(jax.random.fold_in(own_key, 1), (couples,), 0, 1 << 20) % (room + 1)
    sizes = sizes.at[1:1 + 2 * couples:2].set(source_of - moved).at[2:2 + 2 * couples:2].set(sink + moved)
    return sizes[jax.random.permutation(jax.random.fold_in(own_key, 2), count)]


def scatter_about(stream_key, dims, deviation, bound, shards=(), held_as=jnp.bfloat16):
    level = shard_levels(stream_key, dims, shards, -0.22, 0.18) if shards else 1.0
    drawn = jax.random.normal(stream_key, dims, jnp.float32) * deviation * level
    return jnp.minimum(jnp.maximum(drawn, -bound), bound).astype(held_as)


def setup_inputs(seed: int = 0) -> dict:
    key_list = jax.random.split(jax.random.key(seed), 15)
    tokens = scatter_about(key_list[0], (ROWS, LEN, D), 1.0, 6.0, ((0, 2), (1, 16)))
    out_grad = scatter_about(key_list[1], (ROWS, LEN, D), 1.0, 6.0, ((0, 2), (1, 16)))
    doc_lengths = jax.vmap(lambda own: ragged_sizes(own, NDOC, LEN, DOCMAX, 2))(jax.random.split(key_list[2], ROWS)).reshape((ROWS, NDOC)).astype(jnp.int32)
    norm_attn = jnp.clip(1.0 + 0.18 * jax.random.normal(key_list[3], (D,), jnp.float32), 0.099609375, 1.8984375).astype(jnp.bfloat16)
    w_qdown = scatter_about(key_list[4], (D, QL), D ** -0.5, 0.125, ((0, 32),))
    norm_query = jnp.clip(1.0 + 0.18 * jax.random.normal(key_list[5], (QL,), jnp.float32), 0.099609375, 1.8984375).astype(jnp.bfloat16)
    w_qup = scatter_about(key_list[6], (QL, HQ), QL ** -0.5, 0.1875, ((0, 32),))
    w_key = scatter_about(key_list[7], (D, HD), D ** -0.5, 0.125, ((0, 32),))
    w_value = scatter_about(key_list[8], (D, HD), D ** -0.5, 0.125, ((0, 32),))
    w_out = scatter_about(key_list[9], (HQ, D), (HQ // 16) ** -0.5, 0.375, ((1, 32),))
    norm_ffn = jnp.clip(1.0 + 0.18 * jax.random.normal(key_list[10], (D,), jnp.float32), 0.099609375, 1.8984375).astype(jnp.bfloat16)
    w_gate = scatter_about(key_list[11], (D, FF), D ** -0.5, 0.125, ((0, 2), (1, 16)))
    w_up = scatter_about(key_list[12], (D, FF), D ** -0.5, 0.125, ((0, 2), (1, 16)))
    w_down = scatter_about(key_list[13], (FF, D), FF ** -0.5, 0.078125, ((0, 16), (1, 2)))
    return {"tokens": tokens, "out_grad": out_grad, "doc_lengths": doc_lengths, "norm_attn": norm_attn, "w_qdown": w_qdown, "norm_query": norm_query, "w_qup": w_qup, "w_key": w_key, "w_value": w_value, "w_out": w_out, "norm_ffn": norm_ffn, "w_gate": w_gate, "w_up": w_up, "w_down": w_down}


@jax.custom_vjp
def low(v):
    return lax.optimization_barrier(v.astype(jnp.bfloat16)).astype(jnp.float32)

@jax.custom_vjp
def low_back(v):
    return v

def low_keep(v):
    return (low(v), None)

def low_pass(kept, grad):
    return (grad,)

def back_keep(v):
    return (v, None)

def back_low(kept, grad):
    return (low(grad),)
low.defvjp(low_keep, low_pass)
low_back.defvjp(back_keep, back_low)
highest = lax.Precision.HIGHEST
masked = -1e+30
epsilon = 1e-05

def rms_norm(values, gain_vec):
    return values * lax.rsqrt(lax.optimization_barrier(jnp.mean(values * values, axis=-1, keepdims=True)) + epsilon) * gain_vec

def rope_tables(relative, half_dim):
    frequency = 1.0 / 10000.0 ** (jnp.arange(half_dim, dtype=jnp.float32) / half_dim)
    angles = relative.astype(jnp.float32)[..., None] * frequency
    return (jnp.cos(angles), jnp.sin(angles))

def rotate(values, cosine, sine_table):
    half_dim = values.shape[-1] // 2
    front_part = values[..., :half_dim]
    back_part = values[..., half_dim:]
    return jnp.concatenate([front_part * cosine - back_part * sine_table, back_part * cosine + front_part * sine_table], axis=-1)

def doc_layout(lengths, positions):
    doc_ends = jnp.cumsum(lengths).astype(jnp.int32)
    passed = positions[:, None] >= doc_ends[None, :]
    segment = lax.optimization_barrier(jnp.sum(passed.astype(jnp.int32), axis=1)).astype(jnp.int32)
    doc_start = lax.optimization_barrier(jnp.sum(jnp.where(passed, lengths[None, :], 0), axis=1)).astype(jnp.int32)
    return (segment, (positions - doc_start).astype(jnp.int32))

def attend_row(queries, key_rows, value_rows, segment, positions):
    row_length = queries.shape[0]
    blocks = row_length // TOK_DEV
    query_blocks = queries.reshape(blocks, TOK_DEV, HEADS, HD)
    segment_blocks = segment.reshape(blocks, TOK_DEV)
    position_blocks = positions.reshape(blocks, TOK_DEV)

    def score_block(items):
        query_block, query_segment, query_position = items
        scores = jnp.einsum('qhd,kd->qhk', query_block, key_rows, precision=highest) * HD ** (-0.5)
        allowed = (query_segment[:, None] == segment[None, :]) & (positions[None, :] <= query_position[:, None])
        scores = low_back(jnp.where(allowed[:, None, :], scores, masked))
        weights = low(jax.nn.softmax(scores, axis=-1))
        return jnp.einsum('qhk,kd->qhd', weights, value_rows, precision=highest)
    mixed_rows = lax.map(jax.checkpoint(score_block), (query_blocks, segment_blocks, position_blocks))
    return mixed_rows.reshape(row_length, HEADS, HD)

def layer_forward(tokens_f, norm_attn, w_qdown, norm_query, w_qup, w_key, w_value, w_out, norm_ffn, w_gate, w_up, w_down, segment, positions, cosine, sine_table):
    row_count = tokens_f.shape[0]
    row_length = tokens_f.shape[1]
    normed = low(rms_norm(tokens_f, norm_attn))
    latent = low_back(jnp.dot(normed, w_qdown, precision=highest))
    latent_normed = low(rms_norm(latent, norm_query))
    query_raw = low_back(jnp.dot(latent_normed, w_qup, precision=highest)).reshape(row_count, row_length, HEADS, HD)
    queries = low(rotate(query_raw, cosine[:, :, None, :], sine_table[:, :, None, :]))
    key_rows = low(rotate(low_back(jnp.dot(normed, w_key, precision=highest)), cosine, sine_table))
    value_rows = low(low_back(jnp.dot(normed, w_value, precision=highest)))
    attended = lax.map(lambda items: attend_row(*items), (queries, key_rows, value_rows, segment, positions))
    attended = low(low_back(attended)).reshape(row_count, row_length, HEADS * HD)
    branch = low_back(jnp.dot(attended, w_out, precision=highest))
    middle = tokens_f + branch
    normed_ffn = low(rms_norm(middle, norm_ffn))
    gate_act = low_back(jnp.dot(normed_ffn, w_gate, precision=highest))
    upward = low_back(jnp.dot(normed_ffn, w_up, precision=highest))
    hidden = low(jax.nn.silu(gate_act) * upward)
    return middle + low_back(jnp.dot(hidden, w_down, precision=highest))

def reference(tokens, out_grad, doc_lengths, norm_attn, w_qdown, norm_query, w_qup, w_key, w_value, w_out, norm_ffn, w_gate, w_up, w_down):
    row_length = tokens.shape[1]
    positions = jnp.broadcast_to(jnp.arange(row_length, dtype=jnp.int32), (tokens.shape[0], row_length))
    segment, relative = jax.vmap(doc_layout)(doc_lengths, positions)
    cosine, sine_table = rope_tables(relative, HD // 2)
    floats = tuple((item.astype(jnp.float32) for item in (tokens, norm_attn, w_qdown, norm_query, w_qup, w_key, w_value, w_out, norm_ffn, w_gate, w_up, w_down)))

    def forward(*params):
        return layer_forward(*params, segment, positions, cosine, sine_table)
    result, pull_back = jax.vjp(forward, *floats)
    gradients = pull_back(out_grad.astype(jnp.float32))
    return (result.astype(jnp.bfloat16), gradients[0].astype(jnp.bfloat16), gradients[1], gradients[2], gradients[3], gradients[4], gradients[5], gradients[6], gradients[7], gradients[8], gradients[9], gradients[10], gradients[11])
```

```python
import jax
import jax.numpy as jnp
import numpy as np
from jax import lax
from jax.sharding import Mesh, PartitionSpec as P

HEADS = 16
HD = 256
PLANE = 4

masked = -1e30
epsilon = 1e-05
BF = jnp.bfloat16
F32 = jnp.float32


def rms_norm(values, gain_vec):
    return (
        values * lax.rsqrt(jnp.mean(values * values, axis=-1, keepdims=True) + epsilon) * gain_vec
    )


def rope_tables(relative, half_dim):
    frequency = 1.0 / 10000.0 ** (jnp.arange(half_dim, dtype=F32) / half_dim)
    angles = relative.astype(F32)[..., None] * frequency
    return (jnp.cos(angles), jnp.sin(angles))


def rotate(values, cosine, sine_table):
    half_dim = values.shape[-1] // 2
    front = values[..., :half_dim]
    back = values[..., half_dim:]
    return jnp.concatenate(
        [front * cosine - back * sine_table, back * cosine + front * sine_table], axis=-1
    )


def doc_layout(lengths, positions):
    doc_ends = jnp.cumsum(lengths)
    passed = positions[:, None] >= doc_ends[None, :]
    segment = jnp.sum(passed.astype(jnp.int32), axis=1)
    doc_start = jnp.sum(jnp.where(passed, lengths[None, :], 0), axis=1)
    return (segment, positions - doc_start)


def mm(left, right):
    return jnp.dot(left, right, preferred_element_type=F32)


def mm_nt(left, right):
    return jnp.einsum("ik,jk->ij", left, right, preferred_element_type=F32)


def mm_tn(left, right):
    return jnp.einsum("ki,kj->ij", left, right, preferred_element_type=F32)


def shift(value, axis, by=1):
    count = lax.axis_size(axis)
    return lax.ppermute(value, axis, [(i, (i + by) % count) for i in range(count)])


def ring_gather(value, axis):
    pieces = [value]
    for _ in range(lax.axis_size(axis) - 1):
        pieces.append(shift(pieces[-1], axis))
    return pieces


def ring_spread(value, axis):
    return [value] + [shift(value, axis, k) for k in range(1, lax.axis_size(axis))]


def ring_scatter(parts, axis):
    total = parts[1]
    for k in range(2, len(parts) + 1):
        total = shift(total.astype(BF), axis).astype(F32) + parts[k % len(parts)]
    return total


def flip(value, by):
    if by == 3:
        return lax.ppermute(value, ("py", "px"), [(i, i ^ 3) for i in range(PLANE)])
    return lax.ppermute(value, "px" if by == 1 else "py", [(0, 1), (1, 0)])


def halves(value, axis=0):
    half = value.shape[axis] // 2
    return (
        lax.slice_in_dim(value, 0, half, axis=axis),
        lax.slice_in_dim(value, half, 2 * half, axis=axis),
    )


def plane_gather(value, axis=0):
    over_x = flip(value, 1)
    over_y = flip(value, 2)
    first = flip(halves(over_x, axis)[0], 2)
    second = flip(halves(over_y, axis)[1], 1)
    return [value, over_x, over_y, jnp.concatenate([first, second], axis=axis)]


def plane_scatter(parts, axis=0):
    own_a, own_b = halves(parts[0], axis)
    x_a, x_b = halves(parts[1], axis)
    y_a, y_b = halves(parts[2], axis)
    d_a, d_b = halves(parts[3], axis)
    got_xa = flip(d_a.astype(BF), 2)
    got_yb = flip(d_b.astype(BF), 1)
    got_xb = flip(x_b.astype(BF), 1)
    got_ya = flip(y_a.astype(BF), 2)
    fin_a = flip((x_a + got_xa.astype(F32)).astype(BF), 1)
    fin_b = flip((y_b + got_yb.astype(F32)).astype(BF), 2)
    return jnp.concatenate(
        [
            own_a + got_ya.astype(F32) + fin_a.astype(F32),
            own_b + got_xb.astype(F32) + fin_b.astype(F32),
        ],
        axis=axis,
    )


def plane_swap(parts):
    return [parts[0]] + [flip(parts[k], k) for k in range(1, PLANE)]


def pick(stacked, index):
    return lax.dynamic_index_in_dim(stacked, index, 0, keepdims=False)


def plane_order(pieces, place, axis=0):
    stacked = jnp.stack(pieces)
    return jnp.concatenate([pick(stacked, place ^ i) for i in range(PLANE)], axis=axis)


def ring_order(pieces, place, axis=0):
    count = len(pieces)
    stacked = jnp.stack(pieces)
    return jnp.concatenate([pick(stacked, (place - i) % count) for i in range(count)], axis=axis)


def block_of(value, index, size, axis=0):
    return lax.dynamic_slice_in_dim(value, index * size, size, axis)


def swap_features(value, place, count):
    if count == 1:
        return value
    size = value.shape[1] // count
    return jnp.concatenate(
        [block_of(value, (place - k) % count, size, 1) for k in range(count)], axis=1
    )


def plane_ring_weight(parts, spot):
    row, ring, plane = spot
    got = plane_order(plane_swap([pick(parts, plane ^ k) for k in range(PLANE)]), plane)
    got = ring_order(ring_spread(got, "ring"), ring)
    return ring_order(ring_spread(got, "rows"), row)


def plane_ring_gradient(gradient, spot):
    row, ring, plane = spot
    rows, rings = lax.axis_size("rows"), lax.axis_size("ring")
    size = gradient.shape[0] // rows
    total = ring_scatter([block_of(gradient, (row - k) % rows, size) for k in range(rows)], "rows")
    size //= rings
    total = ring_scatter([block_of(total, (ring - k) % rings, size) for k in range(rings)], "ring")
    size //= PLANE
    total = total.astype(BF)
    got = plane_swap([block_of(total, plane ^ k, size) for k in range(PLANE)])
    stacked = jnp.stack(got)
    return [pick(stacked, plane ^ i).astype(F32) for i in range(PLANE)]


def shards(
    tokens,
    out_grad,
    doc_lengths,
    norm_attn,
    w_qdown,
    norm_query,
    w_qup,
    w_key,
    w_value,
    w_out,
    norm_ffn,
    w_gate,
    w_up,
    w_down,
):
    rows, rings = lax.axis_size("rows"), lax.axis_size("ring")
    devices = rows * rings * PLANE
    row = lax.axis_index("rows")
    ring = lax.axis_index("ring")
    plane = lax.axis_index("py") * 2 + lax.axis_index("px")
    spot = (row, ring, plane)
    own_tokens = tokens[0]
    count_local, width = own_tokens.shape
    group = count_local * PLANE
    row_length = group * rings
    heads = HEADS // PLANE
    score_scale = HD ** (-0.5)

    group_tokens = plane_order(plane_gather(own_tokens), plane).astype(F32)

    gains = jnp.concatenate([norm_attn, norm_query, norm_ffn])[None]
    gains = ring_order(ring_spread(gains, "rows"), row)
    part_a, part_q = norm_attn.shape[0], norm_query.shape[0]
    gains = plane_order(plane_swap([gains] * PLANE), plane)
    gains = ring_order(ring_spread(gains, "ring"), ring)
    gains = gains.reshape(rings, PLANE, rows, -1).transpose(2, 0, 1, 3).reshape(devices, -1)
    gains = gains.astype(F32)
    gain_attn = gains[:, :part_a].reshape(-1)
    gain_query = gains[:, part_a : part_a + part_q].reshape(-1)
    gain_ffn = gains[:, part_a + part_q :].reshape(-1)

    latent_width = w_qdown.shape[1] // PLANE
    kv_width = 2 * HD // PLANE
    kv_w = jnp.concatenate([w_key, w_value], axis=1)
    down_parts = jnp.stack(
        [
            jnp.concatenate(
                [
                    w_qdown[:, i * latent_width : (i + 1) * latent_width],
                    kv_w[:, i * kv_width : (i + 1) * kv_width],
                ],
                axis=1,
            )
            for i in range(PLANE)
        ]
    )
    down_w = plane_ring_weight(down_parts, spot)
    up_query = plane_ring_weight(
        w_qup.reshape(w_qup.shape[0], PLANE, -1).transpose(1, 0, 2), spot
    )
    out_t = jnp.transpose(w_out)
    out_proj = plane_ring_weight(
        out_t.reshape(out_t.shape[0], PLANE, -1).transpose(1, 0, 2), spot
    )

    key_positions = jnp.arange(row_length, dtype=jnp.int32)
    key_segment, key_relative = doc_layout(doc_lengths[0], key_positions)
    offset = ring * group
    query_positions = offset + jnp.arange(group, dtype=jnp.int32)
    query_segment = lax.dynamic_slice_in_dim(key_segment, offset, group)
    key_cos, key_sin = rope_tables(key_relative, HD // 2)
    cosine = lax.dynamic_slice_in_dim(key_cos, offset, group)[:, None, :]
    sine_table = lax.dynamic_slice_in_dim(key_sin, offset, group)[:, None, :]
    allowed = (query_segment[:, None] == key_segment[None, :]) & (
        key_positions[None, :] <= query_positions[:, None]
    )

    hidden_w = jnp.stack([jnp.transpose(w_gate), jnp.transpose(w_up), w_down])
    hidden_w = jnp.concatenate(plane_gather(hidden_w, 1), axis=1)
    ffn_w = ring_gather(hidden_w, "rows")
    hidden_units = hidden_w.shape[1]
    feat = hidden_w.shape[2]
    gate_up_w = [w[:2].reshape(2 * hidden_units, feat) for w in ffn_w]
    down_ffn_w = [w[2] for w in ffn_w]

    upstream = out_grad[0]
    upstream_f = upstream.astype(F32)
    ring_upstream = jnp.concatenate(ring_gather(swap_features(upstream, row, rows), "ring"))

    normed_f = rms_norm(group_tokens, gain_attn)
    normed = normed_f.astype(BF)
    projected = mm(normed, down_w).astype(BF)
    key_value = projected[:, latent_width:]
    key_value = ring_order(ring_gather(key_value, "ring"), ring)
    key_value = jnp.stack(plane_gather(key_value))
    key_value = [pick(key_value, plane ^ i) for i in range(PLANE)]
    key_raw = jnp.concatenate(key_value[:2], axis=1).astype(F32)
    all_keys = rotate(key_raw, key_cos, key_sin).astype(BF)
    all_values = jnp.concatenate(key_value[2:], axis=1)

    latent = plane_order(plane_gather(projected[:, :latent_width]), plane, axis=1).astype(F32)
    latent_normed = rms_norm(latent, gain_query).astype(BF)
    query_raw = mm(latent_normed, up_query).reshape(group, heads, HD)
    queries = rotate(query_raw, cosine, sine_table).astype(BF).reshape(group * heads, HD)

    def masked_scores():
        raw_scores = mm_nt(queries, all_keys) * score_scale
        return jnp.where(
            allowed[:, None, :], raw_scores.reshape(group, heads, row_length), masked
        )

    scores = masked_scores()
    row_peak = jnp.max(scores, axis=-1, keepdims=True)
    log_total = row_peak + jnp.log(jnp.sum(jnp.exp(scores - row_peak), axis=-1, keepdims=True))
    probs_bf = jnp.exp(scores - log_total).astype(BF).reshape(group * heads, row_length)
    attended = mm(probs_bf, all_values).reshape(group, heads * HD).astype(BF)
    branch = mm_nt(attended, out_proj)
    branch = plane_scatter([block_of(branch, plane ^ k, count_local) for k in range(PLANE)])
    middle = own_tokens.astype(F32) + branch

    normed2_f, pull_ffn_norm = jax.vjp(rms_norm, middle, gain_ffn)
    normed_ffn = swap_features(normed2_f.astype(BF), row, rows)
    ring_normed = jnp.concatenate(ring_gather(normed_ffn, "ring"))

    def feature_blocks(value):
        return [value[:, k * feat : (k + 1) * feat] for k in range(rows)]

    h2_blocks = feature_blocks(ring_normed)
    dy_blocks = feature_blocks(ring_upstream)
    gate_up = sum(mm_nt(h, w) for h, w in zip(h2_blocks, gate_up_w))
    grad_hidden = sum(mm_nt(d, w) for d, w in zip(dy_blocks, down_ffn_w))

    def gated_unit(both):
        return jax.nn.silu(both[:, :hidden_units]) * both[:, hidden_units:]

    hidden_f, pull_gated = jax.vjp(gated_unit, gate_up)
    hidden = hidden_f.astype(BF)
    grad_gate_up = pull_gated(grad_hidden)[0].astype(BF)

    def ring_parts(blocks):
        whole = jnp.concatenate(blocks, axis=1)
        return [whole[k * count_local : (k + 1) * count_local] for k in range(rings)]

    grad_normed_ffn = ring_scatter(ring_parts([mm(grad_gate_up, w) for w in gate_up_w]), "ring")
    grad_normed_ffn = swap_features(grad_normed_ffn, row, rows)
    output = ring_scatter(ring_parts([mm(hidden, w) for w in down_ffn_w]), "ring")
    output = middle + swap_features(output, row, rows)

    ffn_grad = [
        jnp.concatenate([mm_tn(grad_gate_up, h), mm_tn(hidden, d)])
        for h, d in zip(h2_blocks, dy_blocks)
    ]
    ffn_grad = ring_scatter(ffn_grad, "rows")
    ffn_grad = ffn_grad.reshape(3, PLANE, hidden_units // PLANE, feat)
    ffn_grad = plane_scatter([ffn_grad[:, k] for k in range(PLANE)], axis=1)
    gate_grad = jnp.transpose(ffn_grad[0])
    up_grad = jnp.transpose(ffn_grad[1])
    down_grad = ffn_grad[2]

    grad_middle_norm, grad_gain_ffn = pull_ffn_norm(grad_normed_ffn)
    grad_middle = upstream_f + grad_middle_norm

    branch_grad = plane_order(plane_gather(grad_middle.astype(BF)), plane)
    grad_out_w = plane_ring_gradient(mm_tn(branch_grad, attended), spot)
    grad_out_w = jnp.transpose(jnp.concatenate(grad_out_w, axis=1))
    grad_attended = mm(branch_grad, out_proj).astype(BF).reshape(group * heads, HD)
    scores = masked_scores()
    probs_f = jnp.exp(scores - log_total)
    probs_again = probs_f.astype(BF).reshape(group * heads, row_length)
    grad_probs = mm_nt(grad_attended, all_values).reshape(group, heads, row_length)
    grad_scores = probs_f * (grad_probs - jnp.sum(grad_probs * probs_f, axis=-1, keepdims=True))
    grad_scores = grad_scores.astype(BF).reshape(group * heads, row_length)
    grad_queries = mm(grad_scores, all_keys) * score_scale
    key_part = mm_tn(grad_scores, queries) * score_scale
    value_part = mm_tn(probs_again, grad_attended)
    key_part = rotate(key_part, key_cos, -key_sin)
    kv_parts = jnp.stack(
        [key_part[:, :kv_width], key_part[:, kv_width:]]
        + [value_part[:, :kv_width], value_part[:, kv_width:]]
    )
    kv_grad = plane_scatter([pick(kv_parts, plane ^ k) for k in range(PLANE)])
    kv_grad = ring_scatter(
        [block_of(kv_grad, (ring - k) % rings, group) for k in range(rings)], "ring"
    )

    grad_query_raw = rotate(grad_queries.reshape(group, heads, HD), cosine, -sine_table)
    grad_query_raw = grad_query_raw.reshape(group, heads * HD).astype(BF)
    grad_up_query = plane_ring_gradient(mm_tn(latent_normed, grad_query_raw), spot)
    grad_latent_normed = mm_nt(grad_query_raw, up_query)
    grad_latent_normed = plane_scatter(
        [block_of(grad_latent_normed, plane ^ k, count_local) for k in range(PLANE)]
    )
    own_latent = block_of(latent, plane, count_local)
    pull_latent = jax.vjp(rms_norm, own_latent, gain_query)[1]
    grad_latent, grad_gain_query = pull_latent(grad_latent_normed)
    grad_latent = grad_latent.astype(BF)
    grad_latent = plane_order(
        plane_swap([block_of(grad_latent, plane ^ k, latent_width, 1) for k in range(PLANE)]),
        plane,
    )
    grad_projected = jnp.concatenate([grad_latent, kv_grad.astype(BF)], axis=1)
    grad_down = plane_ring_gradient(mm_tn(normed, grad_projected), spot)
    grad_down_query = jnp.concatenate([p[:, :latent_width] for p in grad_down], axis=1)
    grad_kv_w = jnp.concatenate([p[:, latent_width:] for p in grad_down], axis=1)
    grad_normed = mm_nt(grad_projected, down_w)
    pull_attn_norm = jax.vjp(rms_norm, own_tokens.astype(F32), gain_attn)[1]
    scale = lax.rsqrt(jnp.mean(group_tokens * group_tokens, axis=-1, keepdims=True) + epsilon)
    grad_gain_attn = jnp.sum(grad_normed * group_tokens * scale, axis=0)
    grad_normed = plane_scatter(
        [block_of(grad_normed, plane ^ k, count_local) for k in range(PLANE)]
    )
    grad_input = grad_middle + pull_attn_norm(grad_normed)[0]

    gain_grads = jnp.concatenate(
        [g.reshape(devices, -1) for g in (grad_gain_attn, grad_gain_query, grad_gain_ffn)], axis=1
    ).reshape(rows, rings, PLANE, -1)
    got = ring_scatter_small([pick(gain_grads, (row - k) % rows) for k in range(rows)], "rows")
    got = ring_scatter_small([pick(got, (ring - k) % rings) for k in range(rings)], "ring")
    got = sum(plane_swap([pick(got, plane ^ k) for k in range(PLANE)]))

    return (
        output.astype(BF)[None],
        grad_input.astype(BF)[None],
        got[:part_a],
        grad_down_query,
        got[part_a : part_a + part_q],
        jnp.concatenate(grad_up_query, axis=1),
        grad_kv_w[:, :HD],
        grad_kv_w[:, HD:],
        grad_out_w,
        got[part_a + part_q :],
        gate_grad,
        up_grad,
        down_grad,
    )


def ring_scatter_small(parts, axis):
    return parts[0] + sum(shift(parts[k], axis, -k) for k in range(1, len(parts)))


def solution(mesh):
    rows = mesh.shape["rows"]
    chips = mesh.shape["seq"]
    inner = Mesh(
        np.asarray(mesh.devices).reshape(rows, chips // PLANE, 2, 2), ("rows", "ring", "py", "px")
    )
    seq = ("ring", "py", "px")
    every = ("rows",) + seq
    placed = (
        P("rows", seq, None),
        P("rows", seq, None),
        P("rows", None),
        P(every),
        P(every, None),
        P(every),
        P(every, None),
        P(every, None),
        P(every, None),
        P(None, every),
        P(every),
        P("rows", seq),
        P("rows", seq),
        P(seq, "rows"),
    )
    return jax.shard_map(
        shards,
        mesh=inner,
        in_specs=placed,
        out_specs=(
            P("rows", seq, None),
            P("rows", seq, None),
            P(every),
            P(every, None),
            P(every),
            P(every, None),
            P(every, None),
            P(every, None),
            P(None, every),
            P(every),
            P("rows", seq),
            P("rows", seq),
            P(seq, "rows"),
        ),
        check_vma=False,
    )
```

```python
import jax
import jax.numpy as jnp
import numpy as np
from jax import lax
from jax.experimental import pallas as pl
from jax.experimental.pallas import tpu as pltpu
from jax.sharding import Mesh, PartitionSpec as P

HEADS = 16
HD = 256
PLANE = 4

masked = -1e30
epsilon = 1e-05
BF = jnp.bfloat16
F32 = jnp.float32


def rms_norm(values, gain_vec):
    return (
        values * lax.rsqrt(jnp.mean(values * values, axis=-1, keepdims=True) + epsilon) * gain_vec
    )


def rope_tables(relative, half_dim):
    frequency = 1.0 / 10000.0 ** (jnp.arange(half_dim, dtype=F32) / half_dim)
    angles = relative.astype(F32)[..., None] * frequency
    return (jnp.cos(angles), jnp.sin(angles))


def doc_layout(lengths, positions):
    doc_ends = jnp.cumsum(lengths)
    passed = positions[:, None] >= doc_ends[None, :]
    segment = jnp.sum(passed.astype(jnp.int32), axis=1)
    doc_start = jnp.sum(jnp.where(passed, lengths[None, :], 0), axis=1)
    return (segment, positions - doc_start)


def mm(left, right):
    return jnp.dot(left, right, preferred_element_type=F32)


def mm_nt(left, right):
    return jnp.einsum("ik,jk->ij", left, right, preferred_element_type=F32)


def mm_tn(left, right):
    return jnp.einsum("ki,kj->ij", left, right, preferred_element_type=F32)


def shift(value, axis, by=1):
    count = lax.axis_size(axis)
    return lax.ppermute(value, axis, [(i, (i + by) % count) for i in range(count)])


def ring_gather(value, axis):
    pieces = [value]
    for _ in range(lax.axis_size(axis) - 1):
        pieces.append(shift(pieces[-1], axis))
    return pieces


def ring_spread(value, axis):
    return [value] + [shift(value, axis, k) for k in range(1, lax.axis_size(axis))]


def ring_scatter(parts, axis):
    total = parts[1]
    for k in range(2, len(parts) + 1):
        total = shift(total.astype(BF), axis).astype(F32) + parts[k % len(parts)]
    return total


def flip(value, by):
    if by == 3:
        return lax.ppermute(value, ("py", "px"), [(i, i ^ 3) for i in range(PLANE)])
    return lax.ppermute(value, "px" if by == 1 else "py", [(0, 1), (1, 0)])


def halves(value, axis=0):
    half = value.shape[axis] // 2
    return (
        lax.slice_in_dim(value, 0, half, axis=axis),
        lax.slice_in_dim(value, half, 2 * half, axis=axis),
    )


def plane_gather(value, axis=0):
    over_x = flip(value, 1)
    over_y = flip(value, 2)
    first = flip(halves(over_x, axis)[0], 2)
    second = flip(halves(over_y, axis)[1], 1)
    return [value, over_x, over_y, jnp.concatenate([first, second], axis=axis)]


def plane_scatter(parts, axis=0):
    own_a, own_b = halves(parts[0], axis)
    x_a, x_b = halves(parts[1], axis)
    y_a, y_b = halves(parts[2], axis)
    d_a, d_b = halves(parts[3], axis)
    got_xa = flip(d_a.astype(BF), 2)
    got_yb = flip(d_b.astype(BF), 1)
    got_xb = flip(x_b.astype(BF), 1)
    got_ya = flip(y_a.astype(BF), 2)
    fin_a = flip((x_a + got_xa.astype(F32)).astype(BF), 1)
    fin_b = flip((y_b + got_yb.astype(F32)).astype(BF), 2)
    return jnp.concatenate(
        [
            own_a + got_ya.astype(F32) + fin_a.astype(F32),
            own_b + got_xb.astype(F32) + fin_b.astype(F32),
        ],
        axis=axis,
    )


def plane_swap(parts):
    return [parts[0]] + [flip(parts[k], k) for k in range(1, PLANE)]


def pick(stacked, index):
    return lax.dynamic_index_in_dim(stacked, index, 0, keepdims=False)


def plane_order(pieces, place, axis=0):
    stacked = jnp.stack(pieces)
    return jnp.concatenate([pick(stacked, place ^ i) for i in range(PLANE)], axis=axis)


def ring_order(pieces, place, axis=0):
    count = len(pieces)
    stacked = jnp.stack(pieces)
    return jnp.concatenate([pick(stacked, (place - i) % count) for i in range(count)], axis=axis)


def block_of(value, index, size, axis=0):
    return lax.dynamic_slice_in_dim(value, index * size, size, axis)


def swap_features(value, place, count):
    if count == 1:
        return value
    size = value.shape[1] // count
    return jnp.concatenate(
        [block_of(value, (place - k) % count, size, 1) for k in range(count)], axis=1
    )


def plane_ring_weight(parts, spot):
    row, ring, plane = spot
    got = plane_order(plane_swap([pick(parts, plane ^ k) for k in range(PLANE)]), plane)
    got = ring_order(ring_spread(got, "ring"), ring)
    return ring_order(ring_spread(got, "rows"), row)


def plane_ring_gradient(gradient, spot):
    row, ring, plane = spot
    rows, rings = lax.axis_size("rows"), lax.axis_size("ring")
    size = gradient.shape[0] // rows
    total = ring_scatter([block_of(gradient, (row - k) % rows, size) for k in range(rows)], "rows")
    size //= rings
    total = ring_scatter([block_of(total, (ring - k) % rings, size) for k in range(rings)], "ring")
    size //= PLANE
    total = total.astype(BF)
    got = plane_swap([block_of(total, plane ^ k, size) for k in range(PLANE)])
    stacked = jnp.stack(got)
    return [pick(stacked, plane ^ i).astype(F32) for i in range(PLANE)]


def after(value, *deps):
    return lax.optimization_barrier((value,) + deps)[0]


def params():
    return pltpu.CompilerParams(vmem_limit_bytes=56 * 1024 * 1024)


def dot_nn(left, right):
    return lax.dot_general(left, right, (((1,), (0,)), ((), ())), preferred_element_type=F32)


def dot_nt(left, right):
    return lax.dot_general(left, right, (((1,), (1,)), ((), ())), preferred_element_type=F32)


def dot_tn(left, right):
    return lax.dot_general(left, right, (((0,), (0,)), ((), ())), preferred_element_type=F32)


QB = 256
KB = 512
HALF = HD // 2


def query_bounds(scal, ndoc, block):
    first = scal[1] + block * QB
    positions = first + lax.broadcasted_iota(jnp.int32, (QB, 1), 0)
    starts = jnp.zeros((QB, 1), jnp.int32)
    low_start, end = 0, 0
    for n in range(ndoc):
        end = end + scal[2 + n]
        starts = jnp.where(positions >= end, end, starts)
        low_start = jnp.where(first >= end, end, low_start)
    return positions, starts, lax.div(low_start, KB), lax.div(first + QB - 1, KB) + 1


def attend_kernel(ndoc, scal, q_raw, p0, p1, p2, p3, cos, sin, att, q_out, lse, keys, values):
    head, block = pl.program_id(0), pl.program_id(1)

    @pl.when((head == 0) & (block == 0))
    def _():
        plane = scal[0]
        for i in range(PLANE):
            dest = keys if i < 2 else values
            side = slice((i % 2) * HALF, (i % 2 + 1) * HALF)
            for j, piece in enumerate((p0, p1, p2, p3)):

                @pl.when(plane == (i ^ j))
                def _(dest=dest, side=side, piece=piece):
                    dest[:, side] = piece[...]

        front, back = keys[:, :HALF].astype(F32), keys[:, HALF:].astype(F32)
        keys[:, :HALF] = (front * cos[...] - back * sin[...]).astype(BF)
        keys[:, HALF:] = (back * cos[...] + front * sin[...]).astype(BF)

    rows = pl.ds(pl.multiple_of(scal[1] + block * QB, QB), QB)
    q_cos, q_sin = cos[rows, :], sin[rows, :]
    front, back = q_raw[:, :HALF], q_raw[:, HALF:]
    query = jnp.concatenate(
        [front * q_cos - back * q_sin, back * q_cos + front * q_sin], axis=1
    ).astype(BF)
    query = query * jnp.asarray(HD**-0.5, BF)
    q_out[...] = query
    positions, starts, low, high = query_bounds(scal, ndoc, block)

    def step(kb, carry):
        peak, total, mixed = carry
        span = pl.ds(pl.multiple_of(kb * KB, KB), KB)
        scores = dot_nt(query, keys[span, :])
        where = kb * KB + lax.broadcasted_iota(jnp.int32, (QB, KB), 1)
        scores = jnp.where((where <= positions) & (where >= starts), scores, masked)
        new_peak = jnp.maximum(peak, jnp.max(scores, axis=1, keepdims=True))
        weights = jnp.exp(scores - new_peak)
        keep = jnp.exp(peak - new_peak)
        total = total * keep + jnp.sum(weights, axis=1, keepdims=True)
        mixed = mixed * keep + dot_nn(weights.astype(BF), values[span, :])
        return new_peak, total, mixed

    peak, total, mixed = lax.fori_loop(
        low,
        high,
        step,
        (jnp.full((QB, 1), -3e38, F32), jnp.zeros((QB, 1), F32), jnp.zeros((QB, HD), F32)),
    )
    att[...] = (mixed / total).astype(BF)
    lse[...] = jnp.broadcast_to(peak + jnp.log(total), (QB, 128))


def attend(scal, query_raw, pieces, cos, sin):
    group, wide = query_raw.shape
    length = cos.shape[0]
    heads = wide // HD
    whole = pl.BlockSpec((length, HALF), lambda h, i, s: (0, 0))
    token = pl.BlockSpec((QB, HD), lambda h, i, s: (i, h))
    return pl.pallas_call(
        lambda *refs: attend_kernel(scal.shape[0] - 2, *refs),
        grid_spec=pltpu.PrefetchScalarGridSpec(
            num_scalar_prefetch=1,
            grid=(heads, group // QB),
            in_specs=[token] + [whole] * 6,
            out_specs=[
                token,
                token,
                pl.BlockSpec((QB, 128), lambda h, i, s: (i, h)),
                pl.BlockSpec((length, HD), lambda h, i, s: (0, 0)),
                pl.BlockSpec((length, HD), lambda h, i, s: (0, 0)),
            ],
        ),
        out_shape=[
            jax.ShapeDtypeStruct((group, wide), BF),
            jax.ShapeDtypeStruct((group, wide), BF),
            jax.ShapeDtypeStruct((group, heads * 128), F32),
            jax.ShapeDtypeStruct((length, HD), BF),
            jax.ShapeDtypeStruct((length, HD), BF),
        ],
        compiler_params=params(),
        cost_estimate=pl.CostEstimate(
            flops=4 * group * wide * length, bytes_accessed=8 << 20, transcendentals=0
        ),
        name="attend",
    )(scal, query_raw, *pieces, cos, sin)


def attend_back_kernel(
    ndoc, scal, query, keys, values, lse, att, d_att, cos, sin, d_raw, parts, d_keys, d_values
):
    head, block = pl.program_id(0), pl.program_id(1)

    @pl.when((head == 0) & (block == 0))
    def _():
        d_keys[...] = jnp.zeros_like(d_keys)
        d_values[...] = jnp.zeros_like(d_values)

    positions, starts, low, high = query_bounds(scal, ndoc, block)
    peak = lse[:, :1]
    grad = d_att[...]
    shared = jnp.sum(grad.astype(F32) * att[...].astype(F32), axis=1, keepdims=True)

    def step(kb, d_query):
        span = pl.ds(pl.multiple_of(kb * KB, KB), KB)
        key, value = keys[span, :], values[span, :]
        scores = dot_nt(query[...], key)
        where = kb * KB + lax.broadcasted_iota(jnp.int32, (QB, KB), 1)
        scores = jnp.where((where <= positions) & (where >= starts), scores, masked)
        probs = jnp.exp(scores - peak)
        d_probs = dot_nt(grad, value)
        d_scores = (probs * (d_probs - shared)).astype(BF)
        d_keys[span, :] += dot_tn(d_scores, query[...])
        d_values[span, :] += dot_tn(probs.astype(BF), grad)
        return d_query + dot_nn(d_scores, key)

    d_query = lax.fori_loop(low, high, step, jnp.zeros((QB, HD), F32)) * HD**-0.5
    rows = pl.ds(pl.multiple_of(scal[1] + block * QB, QB), QB)
    q_cos, q_sin = cos[rows, :], sin[rows, :]
    front, back = d_query[:, :HALF], d_query[:, HALF:]
    d_raw[:, :HALF] = (front * q_cos + back * q_sin).astype(BF)
    d_raw[:, HALF:] = (back * q_cos - front * q_sin).astype(BF)

    @pl.when((head == pl.num_programs(0) - 1) & (block == pl.num_programs(1) - 1))
    def _():
        plane = scal[0]
        front, back = d_keys[:, :HALF], d_keys[:, HALF:]
        parts[plane] = front * cos[...] + back * sin[...]
        parts[plane ^ 1] = back * cos[...] - front * sin[...]
        parts[plane ^ 2] = d_values[:, :HALF]
        parts[plane ^ 3] = d_values[:, HALF:]


def attend_back(scal, query, keys, values, lse, att, d_att, cos, sin):
    group, wide = query.shape
    length = cos.shape[0]
    heads = wide // HD
    token = pl.BlockSpec((QB, HD), lambda h, i, s: (i, h))
    table = pl.BlockSpec((length, HALF), lambda h, i, s: (0, 0))
    whole = pl.BlockSpec((length, HD), lambda h, i, s: (0, 0))
    return pl.pallas_call(
        lambda *refs: attend_back_kernel(scal.shape[0] - 2, *refs),
        grid_spec=pltpu.PrefetchScalarGridSpec(
            num_scalar_prefetch=1,
            grid=(heads, group // QB),
            in_specs=[token, whole, whole, pl.BlockSpec((QB, 128), lambda h, i, s: (i, h))]
            + [token, token, table, table],
            out_specs=[token, pl.BlockSpec((PLANE, length, HALF), lambda h, i, s: (0, 0, 0))],
            scratch_shapes=[pltpu.VMEM((length, HD), F32), pltpu.VMEM((length, HD), F32)],
        ),
        out_shape=[
            jax.ShapeDtypeStruct((group, wide), BF),
            jax.ShapeDtypeStruct((PLANE, length, HALF), F32),
        ],
        compiler_params=params(),
        cost_estimate=pl.CostEstimate(
            flops=10 * group * wide * length, bytes_accessed=12 << 20, transcendentals=0
        ),
        name="attend_back",
    )(scal, query, keys, values, lse, att, d_att, cos, sin)


def ffn_kernel(blocks, *refs):
    h_ref, dy_ref = refs[0], refs[1]
    gate_up = refs[2 : 2 + blocks]
    down = refs[2 + blocks : 2 + 2 * blocks]
    hidden, d_gate_up, d_h, out = refs[2 + 2 * blocks :]
    units = hidden.shape[1]
    feat = h_ref.shape[1] // blocks

    def cols(ref, k):
        return ref[:, k * feat : (k + 1) * feat]

    gate = sum(dot_nt(cols(h_ref, k), gate_up[k][:units, :]) for k in range(blocks))
    up = sum(dot_nt(cols(h_ref, k), gate_up[k][units:, :]) for k in range(blocks))
    d_hidden = sum(dot_nt(cols(dy_ref, k), down[k][...]) for k in range(blocks))
    sig = 1.0 / (1.0 + jnp.exp(-gate))
    silu = gate * sig
    hid = (silu * up).astype(BF)
    hidden[...] = hid
    d_gate = (d_hidden * up * (sig + silu * (1.0 - sig))).astype(BF)
    d_up = (d_hidden * silu).astype(BF)
    d_gate_up[:, :units] = d_gate
    d_gate_up[:, units:] = d_up
    for k in range(blocks):
        span = slice(k * feat, (k + 1) * feat)
        d_h[:, span] = dot_nn(d_gate, gate_up[k][:units, :]) + dot_nn(d_up, gate_up[k][units:, :])
        out[:, span] = dot_nn(hid, down[k][...])


def feed_forward(h, dy, gate_up, down):
    count, width = h.shape
    blocks = len(gate_up)
    units, feat = down[0].shape
    tile = min(count, 128)
    token = lambda size: pl.BlockSpec((tile, size), lambda i: (i, 0))
    fixed = lambda size: pl.BlockSpec((size, feat), lambda i: (0, 0), pipeline_mode=pl.Buffered(1))
    return pl.pallas_call(
        lambda *refs: ffn_kernel(blocks, *refs),
        grid=(count // tile,),
        in_specs=[token(width)] * 2 + [fixed(2 * units)] * blocks + [fixed(units)] * blocks,
        out_specs=[token(units), token(2 * units), token(width), token(width)],
        out_shape=[
            jax.ShapeDtypeStruct((count, units), BF),
            jax.ShapeDtypeStruct((count, 2 * units), BF),
            jax.ShapeDtypeStruct((count, width), F32),
            jax.ShapeDtypeStruct((count, width), F32),
        ],
        compiler_params=params(),
        cost_estimate=pl.CostEstimate(
            flops=12 * count * width * units, bytes_accessed=24 << 20, transcendentals=0
        ),
        name="feed_forward",
    )(h, dy, *gate_up, *down)


def shards(
    tokens,
    out_grad,
    doc_lengths,
    norm_attn,
    w_qdown,
    norm_query,
    w_qup,
    w_key,
    w_value,
    w_out,
    norm_ffn,
    w_gate,
    w_up,
    w_down,
):
    rows, rings = lax.axis_size("rows"), lax.axis_size("ring")
    devices = rows * rings * PLANE
    row = lax.axis_index("rows")
    ring = lax.axis_index("ring")
    plane = lax.axis_index("py") * 2 + lax.axis_index("px")
    spot = (row, ring, plane)
    own_tokens = tokens[0]
    count_local, width = own_tokens.shape
    group = count_local * PLANE
    row_length = group * rings

    group_tokens = plane_order(plane_gather(own_tokens), plane).astype(F32)

    gains = jnp.concatenate([norm_attn, norm_query, norm_ffn])[None]
    gains = ring_order(ring_spread(gains, "rows"), row)
    part_a, part_q = norm_attn.shape[0], norm_query.shape[0]
    gains = plane_order(plane_swap([gains] * PLANE), plane)
    gains = ring_order(ring_spread(gains, "ring"), ring)
    gains = gains.reshape(rings, PLANE, rows, -1).transpose(2, 0, 1, 3).reshape(devices, -1)
    gains = gains.astype(F32)
    gain_attn = gains[:, :part_a].reshape(-1)
    gain_query = gains[:, part_a : part_a + part_q].reshape(-1)
    gain_ffn = gains[:, part_a + part_q :].reshape(-1)

    latent_width = w_qdown.shape[1] // PLANE
    kv_width = 2 * HD // PLANE
    kv_w = jnp.concatenate([w_key, w_value], axis=1)
    down_parts = jnp.stack(
        [
            jnp.concatenate(
                [
                    w_qdown[:, i * latent_width : (i + 1) * latent_width],
                    kv_w[:, i * kv_width : (i + 1) * kv_width],
                ],
                axis=1,
            )
            for i in range(PLANE)
        ]
    )
    down_w = plane_ring_weight(down_parts, spot)
    up_query = plane_ring_weight(
        w_qup.reshape(w_qup.shape[0], PLANE, -1).transpose(1, 0, 2), spot
    )
    out_t = jnp.transpose(w_out)
    out_proj = plane_ring_weight(
        out_t.reshape(out_t.shape[0], PLANE, -1).transpose(1, 0, 2), spot
    )

    key_positions = jnp.arange(row_length, dtype=jnp.int32)
    key_relative = doc_layout(doc_lengths[0], key_positions)[1]
    key_cos, key_sin = rope_tables(key_relative, HD // 2)
    scal = jnp.concatenate([jnp.stack([plane, ring * group]), doc_lengths[0]]).astype(jnp.int32)

    gate_w = plane_gather(jnp.stack([jnp.transpose(w_gate), jnp.transpose(w_up)]))
    gate_w = jnp.concatenate(gate_w, axis=1)
    hidden_units, feat = gate_w.shape[1:]
    gate_up_w = ring_gather(gate_w.reshape(2 * hidden_units, feat), "rows")
    down_ffn_w = ring_gather(jnp.concatenate(plane_gather(w_down)), "rows")

    upstream = out_grad[0]
    upstream_f = upstream.astype(F32)
    ring_upstream = ring_gather(swap_features(upstream, row, rows), "ring")

    normed_f = rms_norm(group_tokens, gain_attn)
    normed = normed_f.astype(BF)
    projected = mm(normed, down_w).astype(BF)
    key_value = projected[:, latent_width:]
    key_value = ring_order(ring_gather(key_value, "ring"), ring)
    key_value = plane_gather(key_value)

    latent = plane_order(plane_gather(projected[:, :latent_width]), plane, axis=1).astype(F32)
    latent_normed = rms_norm(latent, gain_query).astype(BF)
    query_raw = mm(latent_normed, up_query)
    attended, queries, log_total, all_keys, all_values = attend(
        scal, query_raw, key_value, key_cos, key_sin
    )
    branch = mm_nt(attended, out_proj)
    branch = plane_scatter([block_of(branch, plane ^ k, count_local) for k in range(PLANE)])
    middle = own_tokens.astype(F32) + branch

    normed2_f, pull_ffn_norm = jax.vjp(rms_norm, middle, gain_ffn)
    normed_ffn = swap_features(normed2_f.astype(BF), row, rows)
    normed_ffn = after(normed_ffn, *ring_upstream)
    ring_normed = ring_gather(normed_ffn, "ring")
    done = []
    chunk = 2
    for first in range(0, rings, chunk):
        h_part = jnp.concatenate(ring_normed[first : first + chunk])
        dy_part = jnp.concatenate(ring_upstream[first : first + chunk])
        done.append((h_part, dy_part) + tuple(feed_forward(h_part, dy_part, gate_up_w, down_ffn_w)))

    def ring_parts(values):
        return [
            values[k // chunk][(k % chunk) * count_local : (k % chunk + 1) * count_local]
            for k in range(rings)
        ]

    grad_normed_ffn = ring_scatter(ring_parts([d[4] for d in done]), "ring")
    outs = after(tuple(d[5] for d in done), grad_normed_ffn)
    grad_normed_ffn = swap_features(grad_normed_ffn, row, rows)
    output = ring_scatter(ring_parts(outs), "ring")
    output = middle + swap_features(output, row, rows)

    ring_h, ring_dy, hidden, grad_gate_up = (
        jnp.concatenate([d[k] for d in done]) for k in range(4)
    )

    def ffn_gradient(left, right, count):
        blocks = [
            mm_tn(left, right[:, k * feat : (k + 1) * feat]).astype(BF) for k in range(rows)
        ]
        total = ring_scatter([b.astype(F32) for b in blocks], "rows").astype(BF)
        total = total.reshape(count, PLANE, -1, feat)
        return plane_scatter(
            [total[:, k].reshape(-1, feat).astype(F32) for k in range(PLANE)]
        )

    down_grad = ffn_gradient(hidden, ring_dy, 1)
    both_grad = ffn_gradient(grad_gate_up, ring_h, 2)
    gate_grad, up_grad = (jnp.transpose(g) for g in halves(both_grad))

    grad_middle_norm, grad_gain_ffn = pull_ffn_norm(grad_normed_ffn)
    grad_middle = upstream_f + grad_middle_norm

    branch_grad = plane_order(plane_gather(grad_middle.astype(BF)), plane)
    grad_out_w = plane_ring_gradient(mm_tn(branch_grad, attended), spot)
    grad_out_w = jnp.transpose(jnp.concatenate(grad_out_w, axis=1))
    grad_attended = mm(branch_grad, out_proj).astype(BF)
    grad_query_raw, kv_parts = attend_back(
        scal,
        queries,
        all_keys,
        all_values,
        log_total,
        attended,
        grad_attended,
        key_cos,
        key_sin,
    )
    kv_grad = plane_scatter([kv_parts[k] for k in range(PLANE)])
    kv_grad = ring_scatter(
        [block_of(kv_grad, (ring - k) % rings, group) for k in range(rings)], "ring"
    )

    grad_up_query = plane_ring_gradient(mm_tn(latent_normed, grad_query_raw), spot)
    grad_latent_normed = mm_nt(grad_query_raw, up_query)
    grad_latent_normed = plane_scatter(
        [block_of(grad_latent_normed, plane ^ k, count_local) for k in range(PLANE)]
    )
    own_latent = block_of(latent, plane, count_local)
    pull_latent = jax.vjp(rms_norm, own_latent, gain_query)[1]
    grad_latent, grad_gain_query = pull_latent(grad_latent_normed)
    grad_latent = grad_latent.astype(BF)
    grad_latent = plane_order(
        plane_swap([block_of(grad_latent, plane ^ k, latent_width, 1) for k in range(PLANE)]),
        plane,
    )
    grad_projected = jnp.concatenate([grad_latent, kv_grad.astype(BF)], axis=1)
    grad_down = plane_ring_gradient(mm_tn(normed, grad_projected), spot)
    grad_down_query = jnp.concatenate([p[:, :latent_width] for p in grad_down], axis=1)
    grad_kv_w = jnp.concatenate([p[:, latent_width:] for p in grad_down], axis=1)
    grad_normed = mm_nt(grad_projected, down_w)
    pull_attn_norm = jax.vjp(rms_norm, own_tokens.astype(F32), gain_attn)[1]
    scale = lax.rsqrt(jnp.mean(group_tokens * group_tokens, axis=-1, keepdims=True) + epsilon)
    grad_gain_attn = jnp.sum(grad_normed * group_tokens * scale, axis=0)
    grad_normed = plane_scatter(
        [block_of(grad_normed, plane ^ k, count_local) for k in range(PLANE)]
    )
    grad_input = grad_middle + pull_attn_norm(grad_normed)[0]

    gain_grads = jnp.concatenate(
        [g.reshape(devices, -1) for g in (grad_gain_attn, grad_gain_query, grad_gain_ffn)], axis=1
    ).reshape(rows, rings, PLANE, -1)
    got = ring_scatter_small([pick(gain_grads, (row - k) % rows) for k in range(rows)], "rows")
    got = ring_scatter_small([pick(got, (ring - k) % rings) for k in range(rings)], "ring")
    got = sum(plane_swap([pick(got, plane ^ k) for k in range(PLANE)]))

    return (
        output.astype(BF)[None],
        grad_input.astype(BF)[None],
        got[:part_a],
        grad_down_query,
        got[part_a : part_a + part_q],
        jnp.concatenate(grad_up_query, axis=1),
        grad_kv_w[:, :HD],
        grad_kv_w[:, HD:],
        grad_out_w,
        got[part_a + part_q :],
        gate_grad,
        up_grad,
        down_grad,
    )


def ring_scatter_small(parts, axis):
    return parts[0] + sum(shift(parts[k], axis, -k) for k in range(1, len(parts)))


def solution(mesh):
    rows = mesh.shape["rows"]
    chips = mesh.shape["seq"]
    inner = Mesh(
        np.asarray(mesh.devices).reshape(rows, chips // PLANE, 2, 2), ("rows", "ring", "py", "px")
    )
    seq = ("ring", "py", "px")
    every = ("rows",) + seq
    placed = (
        P("rows", seq, None),
        P("rows", seq, None),
        P("rows", None),
        P(every),
        P(every, None),
        P(every),
        P(every, None),
        P(every, None),
        P(every, None),
        P(None, every),
        P(every),
        P("rows", seq),
        P("rows", seq),
        P(seq, "rows"),
    )
    return jax.shard_map(
        shards,
        mesh=inner,
        in_specs=placed,
        out_specs=(
            P("rows", seq, None),
            P("rows", seq, None),
            P(every),
            P(every, None),
            P(every),
            P(every, None),
            P(every, None),
            P(every, None),
            P(None, every),
            P(every),
            P("rows", seq),
            P("rows", seq),
            P(seq, "rows"),
        ),
        check_vma=False,
    )
```

```python
import jax
import jax.numpy as jnp
import numpy as np
from jax import lax
from jax.experimental import pallas as pl
from jax.experimental.pallas import tpu as pltpu
from jax.sharding import Mesh, PartitionSpec as P

HEADS = 16
HD = 256
PLANE = 4
EXTRA = 16

masked = -1e30
epsilon = 1e-05
BF = jnp.bfloat16
F32 = jnp.float32


def rms_norm(values, gain_vec):
    return (
        values * lax.rsqrt(jnp.mean(values * values, axis=-1, keepdims=True) + epsilon) * gain_vec
    )


def rope_tables(relative, half_dim):
    frequency = 1.0 / 10000.0 ** (jnp.arange(half_dim, dtype=F32) / half_dim)
    angles = relative.astype(F32)[..., None] * frequency
    return (jnp.cos(angles), jnp.sin(angles))


def doc_layout(lengths, positions):
    doc_ends = jnp.cumsum(lengths)
    passed = positions[:, None] >= doc_ends[None, :]
    segment = jnp.sum(passed.astype(jnp.int32), axis=1)
    doc_start = jnp.sum(jnp.where(passed, lengths[None, :], 0), axis=1)
    return (segment, positions - doc_start)


def mm(left, right):
    return jnp.dot(left, right, preferred_element_type=F32)


def mm_nt(left, right):
    return jnp.einsum("ik,jk->ij", left, right, preferred_element_type=F32)


def mm_tn(left, right):
    return jnp.einsum("ki,kj->ij", left, right, preferred_element_type=F32)


def shift(value, axis, by=1):
    count = lax.axis_size(axis)
    return lax.ppermute(value, axis, [(i, (i + by) % count) for i in range(count)])


def ring_gather(value, axis):
    pieces = [value]
    for _ in range(lax.axis_size(axis) - 1):
        pieces.append(shift(pieces[-1], axis))
    return pieces


def ring_spread(value, axis):
    return [value] + [shift(value, axis, k) for k in range(1, lax.axis_size(axis))]


def ring_scatter(parts, axis):
    total = parts[1]
    for k in range(2, len(parts) + 1):
        total = shift(total.astype(BF), axis).astype(F32) + parts[k % len(parts)]
    return total


def flip(value, by):
    if by == 3:
        return lax.ppermute(value, ("py", "px"), [(i, i ^ 3) for i in range(PLANE)])
    return lax.ppermute(value, "px" if by == 1 else "py", [(0, 1), (1, 0)])


def halves(value, axis=0):
    half = value.shape[axis] // 2
    return (
        lax.slice_in_dim(value, 0, half, axis=axis),
        lax.slice_in_dim(value, half, 2 * half, axis=axis),
    )


def plane_spread(value):
    return [value] + [flip(value, k) for k in range(1, PLANE)]


def plane_sum(parts):
    got = [flip(parts[k].astype(BF), k) for k in range(1, PLANE)]
    return sum((g.astype(F32) for g in got), parts[0].astype(F32))


def token_of(started):
    return shift(started[:8, :128], "rows")


def plane_swap(parts):
    return [parts[0]] + [flip(parts[k], k) for k in range(1, PLANE)]


def pick(stacked, index):
    return lax.dynamic_index_in_dim(stacked, index, 0, keepdims=False)


def place(items, count, unit=None, split=None):
    unit = unit or items[0][0].shape[0]
    columns = items[0][0].shape[1]
    pieces = [v.reshape(-1, unit, columns) for v, _ in items]
    number = len(pieces)
    cuts = [(0, unit)] if split is None else [(0, split), (split, unit)]

    def kernel(slots, *refs):
        outs, sems = refs[number:-1], refs[-1]
        copies = []
        for i in range(number):
            span = pl.ds(slots[i], pieces[i].shape[0])
            for j, (start, stop) in enumerate(cuts):
                source = refs[i] if split is None else refs[i].at[:, pl.ds(start, stop - start)]
                copies.append(pltpu.make_async_copy(source, outs[j].at[span], sems.at[i, j]))
        for copy in copies:
            copy.start()
        for copy in copies:
            copy.wait()

    shapes = [(count, stop - start, columns) for start, stop in cuts]
    outs = pl.pallas_call(
        kernel,
        grid_spec=pltpu.PrefetchScalarGridSpec(
            num_scalar_prefetch=1,
            grid=(1,),
            in_specs=[pl.BlockSpec(memory_space=pl.ANY)] * number,
            out_specs=[pl.BlockSpec(shape, lambda i, s: (0, 0, 0)) for shape in shapes],
            scratch_shapes=[pltpu.SemaphoreType.DMA((number, len(cuts)))],
        ),
        out_shape=[jax.ShapeDtypeStruct(shape, pieces[0].dtype) for shape in shapes],
        compiler_params=params(),
        cost_estimate=pl.CostEstimate(
            flops=0, bytes_accessed=4 * count * unit * columns, transcendentals=0
        ),
        name="place",
    )(jnp.stack([jnp.asarray(slot, jnp.int32) for _, slot in items]), *pieces)
    if split is None:
        return outs[0].reshape(-1, columns)
    return outs


def plane_place(blocks, index):
    return place([(p, index ^ k) for k, p in enumerate(blocks)], PLANE)


def ring_place(pieces, index):
    count = len(pieces)
    return place([(p, (index - k) % count) for k, p in enumerate(pieces)], count)


def block_of(value, index, size, axis=0):
    return lax.dynamic_slice_in_dim(value, index * size, size, axis)


def column_swap(weight, index):
    size = weight.shape[1] // PLANE
    parts = [block_of(weight, index ^ k, size, 1) for k in range(PLANE)]
    return place([(p, index ^ k) for k, p in enumerate(plane_swap(parts))], PLANE)


def rows_place(pieces, row, ring, split=None):
    rings, rows = len(pieces), lax.axis_size("rows")
    unit = pieces[0].shape[0] // PLANE
    own = ring_place(pieces, ring)
    items = [
        (got, (row - j) % rows * rings * PLANE) for j, got in enumerate(ring_spread(own, "rows"))
    ]
    return place(items, rings * rows * PLANE, unit, split)


def row_blocks(left, right, spot, extra=None):
    row, rows = spot[0], lax.axis_size("rows")
    size = left.shape[1] // rows

    def block(k):
        index = (row - k) % rows
        result = mm_tn(block_of(left, index, size, 1), right)
        if extra is not None:
            more = pick(extra, index)
            result = result.reshape(more.shape[0], -1, result.shape[1])
            result = jnp.concatenate([result, more], axis=1).reshape(-1, result.shape[2])
        return result

    return block


def over_rows(block):
    rows = lax.axis_size("rows")
    total = block(1).astype(BF) if rows > 1 else block(0)
    for k in range(2, rows + 1):
        total = shift(total, "rows").astype(F32) + block(k % rows)
        total = total.astype(BF)
    return total


def over_ring(total, spot, pending=()):
    ring, rings = spot[1], lax.axis_size("ring")
    size = total.shape[0] // rings
    total, pending = ring_scatter_bf(
        [block_of(total, (ring - k) % rings, size) for k in range(rings)], pending
    )
    return total.astype(BF), pending


def over_plane(total, spot):
    plane = spot[2]
    size = total.shape[0] // PLANE
    got = plane_swap([block_of(total, plane ^ k, size) for k in range(PLANE)])
    return place([(g, plane ^ k) for k, g in enumerate(got)], PLANE)


def ring_scatter_bf(parts, pending=()):
    count = len(parts)
    total = parts[1]
    for k in range(2, count + 1):
        total = shift(total, "ring").astype(F32) + parts[k % count].astype(F32)
        if k < count:
            total = total.astype(BF)
        if k == 2 and pending:
            total, *pending = tie(total, *pending)
    return total, pending


def tie(value, *deps):
    return lax.optimization_barrier((value,) + deps)


def params():
    return pltpu.CompilerParams(vmem_limit_bytes=56 * 1024 * 1024)


def dot_nn(left, right):
    return lax.dot_general(left, right, (((1,), (0,)), ((), ())), preferred_element_type=F32)


def dot_nt(left, right):
    return lax.dot_general(left, right, (((1,), (1,)), ((), ())), preferred_element_type=F32)


def dot_tn(left, right):
    return lax.dot_general(left, right, (((0,), (0,)), ((), ())), preferred_element_type=F32)


QB = 256
KB = 512
HALF = HD // 2


def query_bounds(scal, ndoc, block):
    first = scal[1] + block * QB
    positions = first + lax.broadcasted_iota(jnp.int32, (QB, 1), 0)
    starts = jnp.zeros((QB, 1), jnp.int32)
    low_start, end = 0, 0
    for n in range(ndoc):
        end = end + scal[2 + n]
        starts = jnp.where(positions >= end, end, starts)
        low_start = jnp.where(first >= end, end, low_start)
    return positions, starts, lax.div(low_start, KB), lax.div(first + QB - 1, KB) + 1


def attend_kernel(ndoc, scal, q_raw, p0, p1, p2, p3, cos, sin, att, q_out, lse, keys, values):
    head, block = pl.program_id(0), pl.program_id(1)

    @pl.when((head == 0) & (block == 0))
    def _():
        plane = scal[0]
        for i in range(PLANE):
            dest = keys if i < 2 else values
            side = slice((i % 2) * HALF, (i % 2 + 1) * HALF)
            for j, piece in enumerate((p0, p1, p2, p3)):

                @pl.when(plane == (i ^ j))
                def _(dest=dest, side=side, piece=piece):
                    dest[:, side] = piece[...]

        front, back = keys[:, :HALF].astype(F32), keys[:, HALF:].astype(F32)
        keys[:, :HALF] = (front * cos[...] - back * sin[...]).astype(BF)
        keys[:, HALF:] = (back * cos[...] + front * sin[...]).astype(BF)

    rows = pl.ds(pl.multiple_of(scal[1] + block * QB, QB), QB)
    q_cos, q_sin = cos[rows, :], sin[rows, :]
    front, back = q_raw[:, :HALF], q_raw[:, HALF:]
    query = jnp.concatenate(
        [front * q_cos - back * q_sin, back * q_cos + front * q_sin], axis=1
    ).astype(BF)
    query = query * jnp.asarray(HD**-0.5, BF)
    q_out[...] = query
    positions, starts, low, high = query_bounds(scal, ndoc, block)

    def step(kb, carry):
        peak, total, mixed = carry
        span = pl.ds(pl.multiple_of(kb * KB, KB), KB)
        scores = dot_nt(query, keys[span, :])
        where = kb * KB + lax.broadcasted_iota(jnp.int32, (QB, KB), 1)
        scores = jnp.where((where <= positions) & (where >= starts), scores, masked)
        new_peak = jnp.maximum(peak, jnp.max(scores, axis=1, keepdims=True))
        weights = jnp.exp(scores - new_peak)
        keep = jnp.exp(peak - new_peak)
        total = total * keep + jnp.sum(weights, axis=1, keepdims=True)
        mixed = mixed * keep + dot_nn(weights.astype(BF), values[span, :])
        return new_peak, total, mixed

    peak, total, mixed = lax.fori_loop(
        low,
        high,
        step,
        (jnp.full((QB, 1), -3e38, F32), jnp.zeros((QB, 1), F32), jnp.zeros((QB, HD), F32)),
    )
    att[...] = (mixed / total).astype(BF)
    lse[...] = jnp.broadcast_to(peak + jnp.log(total), (QB, 128))


def attend(scal, query_raw, pieces, cos, sin):
    group, wide = query_raw.shape
    length = cos.shape[0]
    heads = wide // HD
    whole = pl.BlockSpec((length, HALF), lambda h, i, s: (0, 0))
    token = pl.BlockSpec((QB, HD), lambda h, i, s: (i, h))
    return pl.pallas_call(
        lambda *refs: attend_kernel(scal.shape[0] - 2, *refs),
        grid_spec=pltpu.PrefetchScalarGridSpec(
            num_scalar_prefetch=1,
            grid=(heads, group // QB),
            in_specs=[token] + [whole] * 6,
            out_specs=[
                token,
                token,
                pl.BlockSpec((QB, 128), lambda h, i, s: (i, h)),
                pl.BlockSpec((length, HD), lambda h, i, s: (0, 0)),
                pl.BlockSpec((length, HD), lambda h, i, s: (0, 0)),
            ],
        ),
        out_shape=[
            jax.ShapeDtypeStruct((group, wide), BF),
            jax.ShapeDtypeStruct((group, wide), BF),
            jax.ShapeDtypeStruct((group, heads * 128), F32),
            jax.ShapeDtypeStruct((length, HD), BF),
            jax.ShapeDtypeStruct((length, HD), BF),
        ],
        compiler_params=params(),
        cost_estimate=pl.CostEstimate(
            flops=4 * group * wide * length, bytes_accessed=8 << 20, transcendentals=0
        ),
        name="attend",
    )(scal, query_raw, *pieces, cos, sin)


def attend_back_kernel(
    ndoc, scal, query, keys, values, lse, att, d_att, cos, sin, dep, d_raw, parts, d_keys, d_values
):
    head, block = pl.program_id(0), pl.program_id(1)

    @pl.when((head == 0) & (block == 0))
    def _():
        d_keys[...] = jnp.zeros_like(d_keys)
        d_values[...] = jnp.zeros_like(d_values)

    positions, starts, low, high = query_bounds(scal, ndoc, block)
    peak = lse[:, :1]
    grad = d_att[...]
    shared = jnp.sum(grad.astype(F32) * att[...].astype(F32), axis=1, keepdims=True)

    def step(kb, d_query):
        span = pl.ds(pl.multiple_of(kb * KB, KB), KB)
        key, value = keys[span, :], values[span, :]
        scores = dot_nt(query[...], key)
        where = kb * KB + lax.broadcasted_iota(jnp.int32, (QB, KB), 1)
        scores = jnp.where((where <= positions) & (where >= starts), scores, masked)
        probs = jnp.exp(scores - peak)
        d_probs = dot_nt(grad, value)
        d_scores = (probs * (d_probs - shared)).astype(BF)
        d_keys[span, :] += dot_tn(d_scores, query[...])
        d_values[span, :] += dot_tn(probs.astype(BF), grad)
        return d_query + dot_nn(d_scores, key)

    d_query = lax.fori_loop(low, high, step, jnp.zeros((QB, HD), F32)) * HD**-0.5
    rows = pl.ds(pl.multiple_of(scal[1] + block * QB, QB), QB)
    q_cos, q_sin = cos[rows, :], sin[rows, :]
    front, back = d_query[:, :HALF], d_query[:, HALF:]
    d_raw[:, :HALF] = (front * q_cos + back * q_sin).astype(BF)
    d_raw[:, HALF:] = (back * q_cos - front * q_sin).astype(BF)

    @pl.when((head == pl.num_programs(0) - 1) & (block == pl.num_programs(1) - 1))
    def _():
        plane = scal[0]
        front, back = d_keys[:, :HALF], d_keys[:, HALF:]
        parts[plane] = (front * cos[...] + back * sin[...]).astype(BF)
        parts[plane ^ 1] = (back * cos[...] - front * sin[...]).astype(BF)
        parts[plane ^ 2] = d_values[:, :HALF].astype(BF)
        parts[plane ^ 3] = d_values[:, HALF:].astype(BF)


def attend_back(scal, query, keys, values, lse, att, d_att, cos, sin, dep):
    group, wide = query.shape
    length = cos.shape[0]
    heads = wide // HD
    token = pl.BlockSpec((QB, HD), lambda h, i, s: (i, h))
    table = pl.BlockSpec((length, HALF), lambda h, i, s: (0, 0))
    whole = pl.BlockSpec((length, HD), lambda h, i, s: (0, 0))
    return pl.pallas_call(
        lambda *refs: attend_back_kernel(scal.shape[0] - 2, *refs),
        grid_spec=pltpu.PrefetchScalarGridSpec(
            num_scalar_prefetch=1,
            grid=(heads, group // QB),
            in_specs=[token, whole, whole, pl.BlockSpec((QB, 128), lambda h, i, s: (i, h))]
            + [token, token, table, table, pl.BlockSpec(memory_space=pl.ANY)],
            out_specs=[token, pl.BlockSpec((PLANE, length, HALF), lambda h, i, s: (0, 0, 0))],
            scratch_shapes=[pltpu.VMEM((length, HD), F32), pltpu.VMEM((length, HD), F32)],
        ),
        out_shape=[
            jax.ShapeDtypeStruct((group, wide), BF),
            jax.ShapeDtypeStruct((PLANE, length, HALF), BF),
        ],
        compiler_params=params(),
        cost_estimate=pl.CostEstimate(
            flops=10 * group * wide * length, bytes_accessed=12 << 20, transcendentals=0
        ),
        name="attend_back",
    )(scal, query, keys, values, lse, att, d_att, cos, sin, dep)


def ffn_kernel(chunk, count, blocks, slots, *refs):
    h_refs, dy_ref, w_ref, refs = refs[:count], refs[count], refs[count + 1], refs[count + 2 :]
    if chunk:
        refs = refs[3:]
    acts, h_all, dy_all = refs[:3]
    d_h, out = refs[3 : 3 + count], refs[3 + count : 3 + 2 * count]
    gate_up, down, sems, dy_sems = refs[3 + 2 * count :]
    units = down.shape[1]
    own = units // PLANE
    rows = h_refs[0].shape[0]
    copies = []
    for block in range(blocks):
        for k in range(PLANE):
            at = block * PLANE + k
            for part in range(3):
                source = w_ref.at[pl.ds((3 * at + part) * own, own)]
                if part < 2:
                    dest = gate_up.at[block, pl.ds(part * units + k * own, own)]
                else:
                    dest = down.at[block, pl.ds(k * own, own)]
                copies.append((part, pltpu.make_async_copy(source, dest, sems.at[at, part])))
    for k in range(count):
        source = dy_ref.at[pl.ds(pl.multiple_of(slots[k] * rows, rows), rows)]
        dest = dy_all.at[pl.ds(k * rows, rows)]
        copies.append((2, pltpu.make_async_copy(source, dest, dy_sems.at[k])))
    for part in range(3):
        for kind, copy in copies:
            if kind == part:
                copy.start()
    for k in range(count):
        h_all[k * rows : (k + 1) * rows, :] = h_refs[k][...]
    feat = h_all.shape[1] // blocks

    def cols(ref, k):
        return ref[:, k * feat : (k + 1) * feat]

    def wait(part):
        for kind, copy in copies:
            if kind == part:
                copy.wait()

    wait(0)
    gate = sum(dot_nt(cols(h_all, k), gate_up[k, :units, :]) for k in range(blocks))
    wait(1)
    up = sum(dot_nt(cols(h_all, k), gate_up[k, units:, :]) for k in range(blocks))
    sig = 1.0 / (1.0 + jnp.exp(-gate))
    silu = gate * sig
    hid = (silu * up).astype(BF)
    acts[2] = hid
    wait(2)
    d_hidden = sum(dot_nt(cols(dy_all, k), down[k]) for k in range(blocks))
    d_gate = (d_hidden * up * (sig + silu * (1.0 - sig))).astype(BF)
    d_up = (d_hidden * silu).astype(BF)
    acts[0] = d_gate
    acts[1] = d_up
    for k in range(blocks):
        span = slice(k * feat, (k + 1) * feat)
        grad = dot_nn(d_gate, gate_up[k, :units, :]) + dot_nn(d_up, gate_up[k, units:, :])
        result = dot_nn(hid, down[k])
        for j in range(count):
            d_h[j][:, span] = grad[j * rows : (j + 1) * rows].astype(BF)
            out[j][:, span] = result[j * rows : (j + 1) * rows].astype(BF)


def feed_forward(chunk, chunks, slots, h, dy, weights, held):
    count = len(h)
    rows, width = h[0].shape
    feat = weights.shape[1]
    blocks = width // feat
    units = weights.shape[0] // blocks // 3
    total = rows * count
    whole = pl.BlockSpec((rows, width), lambda i, s: (0, 0))
    anywhere = pl.BlockSpec(memory_space=pl.ANY)
    return pl.pallas_call(
        lambda *refs: ffn_kernel(chunk, count, blocks, *refs),
        grid_spec=pltpu.PrefetchScalarGridSpec(
            num_scalar_prefetch=1,
            grid=(1,),
            in_specs=[whole] * count + [anywhere] * (2 + len(held)),
            out_specs=[pl.BlockSpec((3, total, units), lambda i, s: (0, chunk, 0))]
            + [pl.BlockSpec((total, width), lambda i, s: (chunk, 0))] * 2
            + [whole] * (2 * count),
            scratch_shapes=[
                pltpu.VMEM((blocks, 2 * units, feat), BF),
                pltpu.VMEM((blocks, units, feat), BF),
                pltpu.SemaphoreType.DMA((blocks * PLANE, 3)),
                pltpu.SemaphoreType.DMA((count,)),
            ],
        ),
        out_shape=[jax.ShapeDtypeStruct((3, total * chunks, units), BF)]
        + [jax.ShapeDtypeStruct((total * chunks, width), BF)] * 2
        + [jax.ShapeDtypeStruct((rows, width), BF)] * (2 * count),
        input_output_aliases={3 + count + i: i for i in range(len(held))},
        compiler_params=params(),
        cost_estimate=pl.CostEstimate(
            flops=12 * total * width * units, bytes_accessed=24 << 20, transcendentals=0
        ),
        name="feed_forward",
    )(slots, *h, dy, weights, *held)


def ffn_gradient(acts, h, dy, blocks, dep):
    count, width = h.shape
    units = acts.shape[2]
    feat = width // blocks

    def kernel(left, h_ref, dy_ref, dep_ref, out):
        def store(right):
            result = dot_tn(left[0], right).astype(BF)
            for k in range(PLANE):
                out[0, k, 0] = result[k * (units // PLANE) : (k + 1) * (units // PLANE)]

        part = pl.program_id(1)

        @pl.when(part < 2)
        def _():
            store(h_ref[...])

        @pl.when(part == 2)
        def _():
            store(dy_ref[...])

    right = pl.BlockSpec((count, feat), lambda k, part: (0, k))
    out = pl.pallas_call(
        kernel,
        grid=(blocks, 3),
        in_specs=[pl.BlockSpec((1, count, units), lambda k, part: (part, 0, 0)), right, right]
        + [pl.BlockSpec(memory_space=pl.ANY)],
        out_specs=pl.BlockSpec(
            (1, PLANE, 1, units // PLANE, feat), lambda k, part: (k, 0, part, 0, 0)
        ),
        out_shape=jax.ShapeDtypeStruct((blocks, PLANE, 3, units // PLANE, feat), BF),
        compiler_params=params(),
        cost_estimate=pl.CostEstimate(
            flops=6 * count * width * units, bytes_accessed=24 << 20, transcendentals=0
        ),
        name="ffn_gradient",
    )(acts, h, dy, dep)
    return out.reshape(-1, feat)


def shards(
    tokens,
    out_grad,
    doc_lengths,
    norm_attn,
    w_qdown,
    norm_query,
    w_qup,
    w_key,
    w_value,
    w_out,
    norm_ffn,
    w_gate,
    w_up,
    w_down,
):
    rows, rings = lax.axis_size("rows"), lax.axis_size("ring")
    devices = rows * rings * PLANE
    row = lax.axis_index("rows")
    ring = lax.axis_index("ring")
    plane = lax.axis_index("py") * 2 + lax.axis_index("px")
    spot = (row, ring, plane)
    own_tokens = tokens[0]
    count_local, width = own_tokens.shape
    group = count_local * PLANE
    row_length = group * rings

    latent_width = w_qdown.shape[1] // PLANE
    kv_width = 2 * HD // PLANE
    kv_w = jnp.concatenate([w_key, w_value], axis=1)
    down_w = jnp.concatenate(
        [
            piece
            for i in range(PLANE)
            for piece in (
                w_qdown[:, i * latent_width : (i + 1) * latent_width],
                kv_w[:, i * kv_width : (i + 1) * kv_width],
            )
        ],
        axis=1,
    )
    part_a, part_q = norm_attn.shape[0], norm_query.shape[0]
    gains = jnp.concatenate([norm_attn, norm_query, norm_ffn])
    gain_count = gains.shape[0]
    lanes = latent_width + kv_width
    gains = jnp.tile(jnp.pad(gains, (0, lanes - gain_count)), PLANE)
    gains = jnp.pad(gains[None], ((0, EXTRA - 1), (0, 0)))
    block_rows = down_w.shape[0]
    hidden_axes = ("rows", "py", "px")
    ffn_w = jnp.concatenate([jnp.transpose(w_gate), jnp.transpose(w_up), w_down])
    ffn_w = lax.all_gather(ffn_w, hidden_axes, axis=0, tiled=True)

    down_w = column_swap(jnp.concatenate([down_w, gains]), plane)
    token_blocks = plane_spread(own_tokens)
    down_ring = ring_spread(down_w, "ring")
    other_w = column_swap(jnp.concatenate([w_qup, jnp.transpose(w_out)]), plane)
    other_w = other_w.reshape(PLANE, -1, other_w.shape[1])
    up_rows = w_qup.shape[0]
    up_query = other_w[:, :up_rows].reshape(-1, other_w.shape[2])
    out_proj = other_w[:, up_rows:].reshape(-1, other_w.shape[2])
    up_query, *down_ring = tie(up_query, *down_ring)
    up_ring = ring_gather(up_query, "ring")
    out_proj, *up_ring = tie(out_proj, *up_ring)
    out_proj = rows_place(ring_gather(out_proj, "ring"), row, ring)
    up_query = rows_place(up_ring, row, ring)
    upstream = out_grad[0]
    ring_upstream, ffn_w = tie(upstream, ffn_w)
    ring_upstream = lax.all_gather(ring_upstream, "ring", axis=0, tiled=True)
    down_w, gains = rows_place(down_ring, row, ring, block_rows)
    down_w = down_w.reshape(-1, lanes)
    gains = gains[:, 0, :gain_count].astype(F32)
    gain_attn = gains[:, :part_a].reshape(-1)
    gain_query = gains[:, part_a : part_a + part_q].reshape(-1)
    gain_ffn = gains[:, part_a + part_q :].reshape(-1)

    key_positions = jnp.arange(row_length, dtype=jnp.int32)
    key_relative = doc_layout(doc_lengths[0], key_positions)[1]
    key_cos, key_sin = rope_tables(key_relative, HD // 2)
    scal = jnp.concatenate([jnp.stack([plane, ring * group]), doc_lengths[0]]).astype(jnp.int32)

    group_tokens = plane_place(token_blocks, plane).astype(F32)
    normed = rms_norm(group_tokens, gain_attn).astype(BF)
    projected = mm(normed, down_w).astype(BF)

    key_value = ring_gather(projected[:, latent_width:], "ring")
    latent = plane_spread(projected[:, :latent_width])
    key_value, *latent = tie(ring_place(key_value, ring), *latent)
    latent = jnp.stack(latent)
    latent = jnp.concatenate([pick(latent, plane ^ i) for i in range(PLANE)], axis=1).astype(F32)
    latent_normed = rms_norm(latent, gain_query).astype(BF)
    query_raw = mm(latent_normed, up_query)

    key_value = plane_spread(key_value)
    attended, queries, log_total, all_keys, all_values = attend(
        scal, query_raw, key_value, key_cos, key_sin
    )
    branch = mm_nt(attended, out_proj)
    branch = plane_sum([block_of(branch, plane ^ k, count_local) for k in range(PLANE)])
    middle = own_tokens.astype(F32) + branch

    normed2_f, pull_ffn_norm = jax.vjp(rms_norm, middle, gain_ffn)
    normed_ffn = normed2_f.astype(BF)
    chunk = 2
    chunks = rings // chunk
    held = []
    grad_parts, out_parts = [], []
    ring_normed = [normed_ffn]
    for k in range(1, rings):
        last = ring_normed[-1]
        if k > 1 and k % chunk == chunk - 1:
            last, *held = tie(last, *held)
        ring_normed.append(shift(last, "ring"))
        if k % chunk != chunk - 1:
            continue
        some = slice(k - chunk + 1, k + 1)
        slots = (ring - jnp.arange(k - chunk + 1, k + 1)) % rings
        results = feed_forward(
            k // chunk, chunks, slots, ring_normed[some], ring_upstream, ffn_w, held
        )
        held = results[:3]
        grad_parts += results[3 : 3 + chunk]
        out_parts += results[3 + chunk :]
    grad_normed_ffn, _ = ring_scatter_bf(grad_parts)
    grad_normed_ffn, *out_parts = tie(grad_normed_ffn, *out_parts)
    out_total = out_parts[1]
    for k in range(2, rings):
        out_total = shift(out_total, "ring").astype(F32) + out_parts[k].astype(F32)
        out_total = out_total.astype(BF)
    output = shift(out_total, "ring").astype(F32) + out_parts[0].astype(F32)

    upstream_f = upstream.astype(F32)
    grad_middle_norm, grad_gain_ffn = pull_ffn_norm(grad_normed_ffn)
    grad_middle = upstream_f + grad_middle_norm

    branch_grad = grad_middle.astype(BF)
    branch_blocks = plane_spread(branch_grad)
    ffn_grad = ffn_gradient(*held, rows, token_of(branch_grad))
    ffn_grad = lax.psum_scatter(ffn_grad, hidden_axes, scatter_dimension=0, tiled=True)
    branch_grad = plane_place(branch_blocks, plane)
    grad_attended = mm(branch_grad, out_proj).astype(BF)
    out_block = row_blocks(branch_grad, attended, spot)
    grad_query_raw, kv_parts = attend_back(
        scal,
        queries,
        all_keys,
        all_values,
        log_total,
        attended,
        grad_attended,
        key_cos,
        key_sin,
        out_total,
    )
    grad_out_w = over_rows(out_block)
    kv_parts, output = tie(kv_parts, output)
    grad_out_w, output = tie(grad_out_w, output)
    grad_out_w, _ = over_ring(grad_out_w, spot)
    output = middle + output
    kv_grad = plane_sum([kv_parts[k] for k in range(PLANE)]).astype(BF)
    grad_latent_normed = mm_nt(grad_query_raw, up_query)
    grad_latent_normed, kv_grad = tie(grad_latent_normed, kv_grad)
    kv_grad = ring_scatter(
        [block_of(kv_grad, (ring - k) % rings, group).astype(F32) for k in range(rings)], "ring"
    )
    grad_up_query = over_rows(row_blocks(latent_normed, grad_query_raw, spot))
    grad_up_query, _ = over_ring(grad_up_query, spot)
    grad_latent_normed = plane_sum(
        [block_of(grad_latent_normed, plane ^ k, count_local) for k in range(PLANE)]
    )
    own_latent = block_of(latent, plane, count_local)
    pull_latent = jax.vjp(rms_norm, own_latent, gain_query)[1]
    grad_latent, grad_gain_query = pull_latent(grad_latent_normed)
    grad_latent = grad_latent.astype(BF)
    grad_latent = plane_swap(
        [block_of(grad_latent, plane ^ k, latent_width, 1) for k in range(PLANE)]
    )
    grad_latent = place([(g, plane ^ k) for k, g in enumerate(grad_latent)], PLANE)
    grad_projected = jnp.concatenate([grad_latent, kv_grad.astype(BF)], axis=1)
    grad_projected, grad_out_w, grad_up_query = tie(grad_projected, grad_out_w, grad_up_query)
    grad_normed = mm_nt(grad_projected, down_w)
    pull_attn_norm = jax.vjp(rms_norm, own_tokens.astype(F32), gain_attn)[1]
    scale = lax.rsqrt(jnp.mean(group_tokens * group_tokens, axis=-1, keepdims=True) + epsilon)
    grad_gain_attn = jnp.sum(grad_normed * group_tokens * scale, axis=0)
    gain_grads = jnp.concatenate(
        [g.reshape(devices, -1) for g in (grad_gain_attn, grad_gain_query, grad_gain_ffn)], axis=1
    )
    gain_grads = jnp.pad(gain_grads[:, None], ((0, 0), (0, EXTRA - 1), (0, lanes - gain_count)))
    gain_grads = gain_grads.reshape(rows, rings * PLANE, EXTRA, lanes)
    grad_down = over_rows(row_blocks(normed, grad_projected, spot, gain_grads))
    grad_down, (grad_up_query, grad_out_w) = over_ring(
        grad_down, spot, (grad_up_query, grad_out_w)
    )
    grad_up_query = beside(over_plane(grad_up_query, spot)).astype(F32)
    grad_out_w = jnp.transpose(beside(over_plane(grad_out_w, spot)).astype(F32))
    grad_down = over_plane(grad_down, spot)
    grad_down = grad_down.reshape(PLANE, -1, grad_down.shape[1]).astype(F32)
    grad_gains = jnp.sum(grad_down[:, block_rows, :gain_count], axis=0)
    grad_down = grad_down[:, :block_rows]
    grad_down_query = jnp.concatenate([p[:, :latent_width] for p in grad_down], axis=1)
    grad_kv_w = jnp.concatenate([p[:, latent_width:] for p in grad_down], axis=1)
    grad_normed = plane_sum(
        [block_of(grad_normed, plane ^ k, count_local) for k in range(PLANE)]
    )
    grad_input = grad_middle + pull_attn_norm(grad_normed)[0]
    ffn_grad = ffn_grad.astype(F32).reshape(3, -1, ffn_grad.shape[1])
    gate_grad, up_grad, down_grad = jnp.transpose(ffn_grad[0]), jnp.transpose(ffn_grad[1]), ffn_grad[2]

    return (
        output.astype(BF)[None],
        grad_input.astype(BF)[None],
        grad_gains[:part_a],
        grad_down_query,
        grad_gains[part_a : part_a + part_q],
        grad_up_query,
        grad_kv_w[:, :HD],
        grad_kv_w[:, HD:],
        grad_out_w,
        grad_gains[part_a + part_q :],
        gate_grad,
        up_grad,
        down_grad,
    )


def beside(stacked):
    blocks = stacked.reshape(PLANE, -1, stacked.shape[1])
    return jnp.concatenate(list(blocks), axis=1)


def solution(mesh):
    rows = mesh.shape["rows"]
    chips = mesh.shape["seq"]
    inner = Mesh(
        np.asarray(mesh.devices).reshape(rows, chips // PLANE, 2, 2), ("rows", "ring", "py", "px")
    )
    seq = ("ring", "py", "px")
    every = ("rows",) + seq
    placed = (
        P("rows", seq, None),
        P("rows", seq, None),
        P("rows", None),
        P(every),
        P(every, None),
        P(every),
        P(every, None),
        P(every, None),
        P(every, None),
        P(None, every),
        P(every),
        P("rows", seq),
        P("rows", seq),
        P(seq, "rows"),
    )
    return jax.shard_map(
        shards,
        mesh=inner,
        in_specs=placed,
        out_specs=(
            P("rows", seq, None),
            P("rows", seq, None),
            P(every),
            P(every, None),
            P(every),
            P(every, None),
            P(every, None),
            P(every, None),
            P(None, every),
            P(every),
            P("rows", seq),
            P("rows", seq),
            P(seq, "rows"),
        ),
        check_vma=False,
    )
```

```python
import jax
import jax.numpy as jnp
import numpy as np
from jax import lax
from jax.experimental import pallas as pl
from jax.experimental.pallas import tpu as pltpu
from jax.sharding import Mesh, PartitionSpec as P

HEADS = 16
HD = 256
PLANE = 4
EXTRA = 16

masked = -1e30
epsilon = 1e-05
BF = jnp.bfloat16
F32 = jnp.float32


def rms_norm(values, gain_vec):
    return (
        values * lax.rsqrt(jnp.mean(values * values, axis=-1, keepdims=True) + epsilon) * gain_vec
    )


def rope_tables(relative, half_dim):
    frequency = 1.0 / 10000.0 ** (jnp.arange(half_dim, dtype=F32) / half_dim)
    angles = relative.astype(F32)[..., None] * frequency
    return (jnp.cos(angles), jnp.sin(angles))


def doc_layout(lengths, positions):
    doc_ends = jnp.cumsum(lengths)
    passed = positions[:, None] >= doc_ends[None, :]
    segment = jnp.sum(passed.astype(jnp.int32), axis=1)
    doc_start = jnp.sum(jnp.where(passed, lengths[None, :], 0), axis=1)
    return (segment, positions - doc_start)


def mm(left, right):
    return jnp.dot(left, right, preferred_element_type=F32)


def mm_nt(left, right):
    return jnp.einsum("ik,jk->ij", left, right, preferred_element_type=F32)


def mm_tn(left, right):
    return jnp.einsum("ki,kj->ij", left, right, preferred_element_type=F32)


def shift(value, axis, by=1):
    count = lax.axis_size(axis)
    return lax.ppermute(value, axis, [(i, (i + by) % count) for i in range(count)])


def ring_gather(value, axis):
    pieces = [value]
    for _ in range(lax.axis_size(axis) - 1):
        pieces.append(shift(pieces[-1], axis))
    return pieces


def ring_spread(value, axis):
    return [value] + [shift(value, axis, k) for k in range(1, lax.axis_size(axis))]


def flip(value, by):
    if by == 3:
        return lax.ppermute(value, ("py", "px"), [(i, i ^ 3) for i in range(PLANE)])
    return lax.ppermute(value, "px" if by == 1 else "py", [(0, 1), (1, 0)])


def halves(value, axis=0):
    half = value.shape[axis] // 2
    return (
        lax.slice_in_dim(value, 0, half, axis=axis),
        lax.slice_in_dim(value, half, 2 * half, axis=axis),
    )


def plane_spread(value):
    return [value] + [flip(value, k) for k in range(1, PLANE)]


def plane_sum(parts):
    got = [flip(parts[k].astype(BF), k) for k in range(1, PLANE)]
    return sum((g.astype(F32) for g in got), parts[0].astype(F32))


def plane_swap(parts):
    return [parts[0]] + [flip(parts[k], k) for k in range(1, PLANE)]


def pick(stacked, index):
    return lax.dynamic_index_in_dim(stacked, index, 0, keepdims=False)


def place(items, count, unit=None, split=None):
    unit = unit or items[0][0].shape[0]
    columns = items[0][0].shape[1]
    pieces = [v.reshape(-1, unit, columns) for v, _ in items]
    number = len(pieces)
    cuts = [(0, unit)] if split is None else [(0, split), (split, unit)]

    def kernel(slots, *refs):
        outs, sems = refs[number:-1], refs[-1]
        copies = []
        for i in range(number):
            span = pl.ds(slots[i], pieces[i].shape[0])
            for j, (start, stop) in enumerate(cuts):
                source = refs[i] if split is None else refs[i].at[:, pl.ds(start, stop - start)]
                copies.append(pltpu.make_async_copy(source, outs[j].at[span], sems.at[i, j]))
        for copy in copies:
            copy.start()
        for copy in copies:
            copy.wait()

    shapes = [(count, stop - start, columns) for start, stop in cuts]
    outs = pl.pallas_call(
        kernel,
        grid_spec=pltpu.PrefetchScalarGridSpec(
            num_scalar_prefetch=1,
            grid=(1,),
            in_specs=[pl.BlockSpec(memory_space=pl.ANY)] * number,
            out_specs=[pl.BlockSpec(shape, lambda i, s: (0, 0, 0)) for shape in shapes],
            scratch_shapes=[pltpu.SemaphoreType.DMA((number, len(cuts)))],
        ),
        out_shape=[jax.ShapeDtypeStruct(shape, pieces[0].dtype) for shape in shapes],
        compiler_params=params(),
        cost_estimate=pl.CostEstimate(
            flops=0, bytes_accessed=4 * count * unit * columns, transcendentals=0
        ),
        name="place",
    )(jnp.stack([jnp.asarray(slot, jnp.int32) for _, slot in items]), *pieces)
    if split is None:
        return outs[0].reshape(-1, columns)
    return outs


def plane_place(blocks, index):
    return place([(p, index ^ k) for k, p in enumerate(blocks)], PLANE)


def ring_place(pieces, index):
    count = len(pieces)
    return place([(p, (index - k) % count) for k, p in enumerate(pieces)], count)


def block_of(value, index, size, axis=0):
    return lax.dynamic_slice_in_dim(value, index * size, size, axis)


def column_swap(weight, index):
    size = weight.shape[1] // PLANE
    parts = [block_of(weight, index ^ k, size, 1) for k in range(PLANE)]
    return place([(p, index ^ k) for k, p in enumerate(plane_swap(parts))], PLANE)


def rows_place(pieces, row, ring, split=None):
    rings, rows = len(pieces), lax.axis_size("rows")
    unit = pieces[0].shape[0] // PLANE
    own = ring_place(pieces, ring)
    items = [
        (got, (row - j) % rows * rings * PLANE) for j, got in enumerate(ring_spread(own, "rows"))
    ]
    return place(items, rings * rows * PLANE, unit, split)


def row_blocks(left, right, spot, extra=None):
    row, rows = spot[0], lax.axis_size("rows")
    size = left.shape[1] // rows

    def block(k):
        index = (row - k) % rows
        result = mm_tn(block_of(left, index, size, 1), right)
        if extra is not None:
            more = pick(extra, index)
            result = result.reshape(more.shape[0], -1, result.shape[1])
            result = jnp.concatenate([result, more], axis=1).reshape(-1, result.shape[2])
        return result

    return block


def over_rows(block):
    rows = lax.axis_size("rows")
    total = block(1).astype(BF) if rows > 1 else block(0)
    for k in range(2, rows + 1):
        total = shift(total, "rows").astype(F32) + block(k % rows)
        total = total.astype(BF)
    return total


def ring_parts(total, spot):
    ring, rings = spot[1], lax.axis_size("ring")
    size = total.shape[0] // rings
    return [block_of(total, (ring - k) % rings, size) for k in range(rings)]


def over_plane(total, spot, split):
    plane = spot[2]
    size = total.shape[0] // PLANE
    got = plane_swap([block_of(total, plane ^ k, size) for k in range(PLANE)])
    return place([(g, plane ^ k) for k, g in enumerate(got)], PLANE, None, split)


def ring_steps(parts, first, last, total=None):
    count = len(parts)
    total = parts[1] if total is None else total
    for k in range(first + 1, last + 2):
        total = shift(total, "ring").astype(F32) + parts[k % count].astype(F32)
        if k < count:
            total = total.astype(BF)
    return total


def tie(value, *deps):
    return lax.optimization_barrier((value,) + deps)


def params():
    return pltpu.CompilerParams(vmem_limit_bytes=56 * 1024 * 1024)


def dot_nn(left, right):
    return lax.dot_general(left, right, (((1,), (0,)), ((), ())), preferred_element_type=F32)


def dot_nt(left, right):
    return lax.dot_general(left, right, (((1,), (1,)), ((), ())), preferred_element_type=F32)


def dot_tn(left, right):
    return lax.dot_general(left, right, (((0,), (0,)), ((), ())), preferred_element_type=F32)


QB = 256
KB = 512
HALF = HD // 2


def query_bounds(scal, ndoc, block):
    first = scal[1] + block * QB
    positions = first + lax.broadcasted_iota(jnp.int32, (QB, 1), 0)
    starts = jnp.zeros((QB, 1), jnp.int32)
    low_start, end = 0, 0
    for n in range(ndoc):
        end = end + scal[2 + n]
        starts = jnp.where(positions >= end, end, starts)
        low_start = jnp.where(first >= end, end, low_start)
    return positions, starts, lax.div(low_start, KB), lax.div(first + QB - 1, KB) + 1


def attend_kernel(ndoc, scal, q_raw, p0, p1, p2, p3, cos, sin, att, q_out, lse, keys, values):
    head, block = pl.program_id(0), pl.program_id(1)

    @pl.when((head == 0) & (block == 0))
    def _():
        plane = scal[0]
        for i in range(PLANE):
            dest = keys if i < 2 else values
            side = slice((i % 2) * HALF, (i % 2 + 1) * HALF)
            for j, piece in enumerate((p0, p1, p2, p3)):

                @pl.when(plane == (i ^ j))
                def _(dest=dest, side=side, piece=piece):
                    dest[:, side] = piece[...]

        front, back = keys[:, :HALF].astype(F32), keys[:, HALF:].astype(F32)
        keys[:, :HALF] = (front * cos[...] - back * sin[...]).astype(BF)
        keys[:, HALF:] = (back * cos[...] + front * sin[...]).astype(BF)

    rows = pl.ds(pl.multiple_of(scal[1] + block * QB, QB), QB)
    q_cos, q_sin = cos[rows, :], sin[rows, :]
    front, back = q_raw[:, :HALF], q_raw[:, HALF:]
    query = jnp.concatenate(
        [front * q_cos - back * q_sin, back * q_cos + front * q_sin], axis=1
    ).astype(BF)
    query = query * jnp.asarray(HD**-0.5, BF)
    q_out[...] = query
    positions, starts, low, high = query_bounds(scal, ndoc, block)

    def step(kb, carry):
        peak, total, mixed = carry
        span = pl.ds(pl.multiple_of(kb * KB, KB), KB)
        scores = dot_nt(query, keys[span, :])
        where = kb * KB + lax.broadcasted_iota(jnp.int32, (QB, KB), 1)
        scores = jnp.where((where <= positions) & (where >= starts), scores, masked)
        new_peak = jnp.maximum(peak, jnp.max(scores, axis=1, keepdims=True))
        weights = jnp.exp(scores - new_peak)
        keep = jnp.exp(peak - new_peak)
        total = total * keep + jnp.sum(weights, axis=1, keepdims=True)
        mixed = mixed * keep + dot_nn(weights.astype(BF), values[span, :])
        return new_peak, total, mixed

    peak, total, mixed = lax.fori_loop(
        low,
        high,
        step,
        (jnp.full((QB, 1), -3e38, F32), jnp.zeros((QB, 1), F32), jnp.zeros((QB, HD), F32)),
    )
    att[...] = (mixed / total).astype(BF)
    lse[...] = jnp.broadcast_to(peak + jnp.log(total), (QB, 128))


def attend(scal, query_raw, pieces, cos, sin):
    group, wide = query_raw.shape
    length = cos.shape[0]
    heads = wide // HD
    whole = pl.BlockSpec((length, HALF), lambda h, i, s: (0, 0))
    token = pl.BlockSpec((QB, HD), lambda h, i, s: (i, h))
    return pl.pallas_call(
        lambda *refs: attend_kernel(scal.shape[0] - 2, *refs),
        grid_spec=pltpu.PrefetchScalarGridSpec(
            num_scalar_prefetch=1,
            grid=(heads, group // QB),
            in_specs=[token] + [whole] * 6,
            out_specs=[
                token,
                token,
                pl.BlockSpec((QB, 128), lambda h, i, s: (i, h)),
                pl.BlockSpec((length, HD), lambda h, i, s: (0, 0)),
                pl.BlockSpec((length, HD), lambda h, i, s: (0, 0)),
            ],
        ),
        out_shape=[
            jax.ShapeDtypeStruct((group, wide), BF),
            jax.ShapeDtypeStruct((group, wide), BF),
            jax.ShapeDtypeStruct((group, heads * 128), F32),
            jax.ShapeDtypeStruct((length, HD), BF),
            jax.ShapeDtypeStruct((length, HD), BF),
        ],
        compiler_params=params(),
        cost_estimate=pl.CostEstimate(
            flops=4 * group * wide * length, bytes_accessed=8 << 20, transcendentals=0
        ),
        name="attend",
    )(scal, query_raw, *pieces, cos, sin)


def attend_back_kernel(
    ndoc, scal, query, keys, values, lse, att, d_att, cos, sin, dep, d_raw, parts, d_keys, d_values
):
    head, block = pl.program_id(0), pl.program_id(1)

    @pl.when((head == 0) & (block == 0))
    def _():
        d_keys[...] = jnp.zeros_like(d_keys)
        d_values[...] = jnp.zeros_like(d_values)

    positions, starts, low, high = query_bounds(scal, ndoc, block)
    peak = lse[:, :1]
    grad = d_att[...]
    shared = jnp.sum(grad.astype(F32) * att[...].astype(F32), axis=1, keepdims=True)

    def step(kb, d_query):
        span = pl.ds(pl.multiple_of(kb * KB, KB), KB)
        key, value = keys[span, :], values[span, :]
        scores = dot_nt(query[...], key)
        where = kb * KB + lax.broadcasted_iota(jnp.int32, (QB, KB), 1)
        scores = jnp.where((where <= positions) & (where >= starts), scores, masked)
        probs = jnp.exp(scores - peak)
        d_probs = dot_nt(grad, value)
        d_scores = (probs * (d_probs - shared)).astype(BF)
        d_keys[span, :] += dot_tn(d_scores, query[...])
        d_values[span, :] += dot_tn(probs.astype(BF), grad)
        return d_query + dot_nn(d_scores, key)

    d_query = lax.fori_loop(low, high, step, jnp.zeros((QB, HD), F32)) * HD**-0.5
    rows = pl.ds(pl.multiple_of(scal[1] + block * QB, QB), QB)
    q_cos, q_sin = cos[rows, :], sin[rows, :]
    front, back = d_query[:, :HALF], d_query[:, HALF:]
    d_raw[:, :HALF] = (front * q_cos + back * q_sin).astype(BF)
    d_raw[:, HALF:] = (back * q_cos - front * q_sin).astype(BF)

    @pl.when((head == pl.num_programs(0) - 1) & (block == pl.num_programs(1) - 1))
    def _():
        plane = scal[0]
        front, back = d_keys[:, :HALF], d_keys[:, HALF:]
        parts[plane] = (front * cos[...] + back * sin[...]).astype(BF)
        parts[plane ^ 1] = (back * cos[...] - front * sin[...]).astype(BF)
        parts[plane ^ 2] = d_values[:, :HALF].astype(BF)
        parts[plane ^ 3] = d_values[:, HALF:].astype(BF)


def attend_back(scal, query, keys, values, lse, att, d_att, cos, sin, dep):
    group, wide = query.shape
    length = cos.shape[0]
    heads = wide // HD
    token = pl.BlockSpec((QB, HD), lambda h, i, s: (i, h))
    table = pl.BlockSpec((length, HALF), lambda h, i, s: (0, 0))
    whole = pl.BlockSpec((length, HD), lambda h, i, s: (0, 0))
    return pl.pallas_call(
        lambda *refs: attend_back_kernel(scal.shape[0] - 2, *refs),
        grid_spec=pltpu.PrefetchScalarGridSpec(
            num_scalar_prefetch=1,
            grid=(heads, group // QB),
            in_specs=[token, whole, whole, pl.BlockSpec((QB, 128), lambda h, i, s: (i, h))]
            + [token, token, table, table, pl.BlockSpec(memory_space=pl.ANY)],
            out_specs=[token, pl.BlockSpec((PLANE, length, HALF), lambda h, i, s: (0, 0, 0))],
            scratch_shapes=[pltpu.VMEM((length, HD), F32), pltpu.VMEM((length, HD), F32)],
        ),
        out_shape=[
            jax.ShapeDtypeStruct((group, wide), BF),
            jax.ShapeDtypeStruct((PLANE, length, HALF), BF),
        ],
        compiler_params=params(),
        cost_estimate=pl.CostEstimate(
            flops=10 * group * wide * length, bytes_accessed=12 << 20, transcendentals=0
        ),
        name="attend_back",
    )(scal, query, keys, values, lse, att, d_att, cos, sin, dep)


def ffn_kernel(chunk, count, blocks, slots, *refs):
    h_refs, dy_ref, w_ref, refs = refs[:count], refs[count], refs[count + 1], refs[count + 2 :]
    if chunk:
        refs = refs[3:]
    acts, h_all, dy_all = refs[:3]
    d_h, out = refs[3 : 3 + count], refs[3 + count : 3 + 2 * count]
    gate_up, down, sems, dy_sems = refs[3 + 2 * count :]
    units = down.shape[1]
    own = units // PLANE
    rows = h_refs[0].shape[0]
    copies = []
    for block in range(blocks):
        for k in range(PLANE):
            at = block * PLANE + k
            for part in range(3):
                source = w_ref.at[pl.ds((3 * at + part) * own, own)]
                if part < 2:
                    dest = gate_up.at[block, pl.ds(part * units + k * own, own)]
                else:
                    dest = down.at[block, pl.ds(k * own, own)]
                copies.append((part, pltpu.make_async_copy(source, dest, sems.at[at, part])))
    for k in range(count):
        source = dy_ref.at[pl.ds(pl.multiple_of(slots[k] * rows, rows), rows)]
        dest = dy_all.at[pl.ds(k * rows, rows)]
        copies.append((2, pltpu.make_async_copy(source, dest, dy_sems.at[k])))
    for part in range(3):
        for kind, copy in copies:
            if kind == part:
                copy.start()
    for k in range(count):
        h_all[k * rows : (k + 1) * rows, :] = h_refs[k][...]
    feat = h_all.shape[1] // blocks

    def cols(ref, k):
        return ref[:, k * feat : (k + 1) * feat]

    def wait(part):
        for kind, copy in copies:
            if kind == part:
                copy.wait()

    wait(0)
    gate = sum(dot_nt(cols(h_all, k), gate_up[k, :units, :]) for k in range(blocks))
    wait(1)
    up = sum(dot_nt(cols(h_all, k), gate_up[k, units:, :]) for k in range(blocks))
    sig = 1.0 / (1.0 + jnp.exp(-gate))
    silu = gate * sig
    hid = (silu * up).astype(BF)
    acts[2] = hid
    wait(2)
    d_hidden = sum(dot_nt(cols(dy_all, k), down[k]) for k in range(blocks))
    d_gate = (d_hidden * up * (sig + silu * (1.0 - sig))).astype(BF)
    d_up = (d_hidden * silu).astype(BF)
    acts[0] = d_gate
    acts[1] = d_up
    for k in range(blocks):
        span = slice(k * feat, (k + 1) * feat)
        grad = dot_nn(d_gate, gate_up[k, :units, :]) + dot_nn(d_up, gate_up[k, units:, :])
        result = dot_nn(hid, down[k])
        for j in range(count):
            d_h[j][:, span] = grad[j * rows : (j + 1) * rows].astype(BF)
            out[j][:, span] = result[j * rows : (j + 1) * rows].astype(BF)


def feed_forward(chunk, chunks, slots, h, dy, weights, held):
    count = len(h)
    rows, width = h[0].shape
    feat = weights.shape[1]
    blocks = width // feat
    units = weights.shape[0] // blocks // 3
    total = rows * count
    whole = pl.BlockSpec((rows, width), lambda i, s: (0, 0))
    anywhere = pl.BlockSpec(memory_space=pl.ANY)
    return pl.pallas_call(
        lambda *refs: ffn_kernel(chunk, count, blocks, *refs),
        grid_spec=pltpu.PrefetchScalarGridSpec(
            num_scalar_prefetch=1,
            grid=(1,),
            in_specs=[whole] * count + [anywhere] * (2 + len(held)),
            out_specs=[pl.BlockSpec((3, total, units), lambda i, s: (0, chunk, 0))]
            + [pl.BlockSpec((total, width), lambda i, s: (chunk, 0))] * 2
            + [whole] * (2 * count),
            scratch_shapes=[
                pltpu.VMEM((blocks, 2 * units, feat), BF),
                pltpu.VMEM((blocks, units, feat), BF),
                pltpu.SemaphoreType.DMA((blocks * PLANE, 3)),
                pltpu.SemaphoreType.DMA((count,)),
            ],
        ),
        out_shape=[jax.ShapeDtypeStruct((3, total * chunks, units), BF)]
        + [jax.ShapeDtypeStruct((total * chunks, width), BF)] * 2
        + [jax.ShapeDtypeStruct((rows, width), BF)] * (2 * count),
        input_output_aliases={3 + count + i: i for i in range(len(held))},
        compiler_params=params(),
        cost_estimate=pl.CostEstimate(
            flops=12 * total * width * units, bytes_accessed=24 << 20, transcendentals=0
        ),
        name="feed_forward",
    )(slots, *h, dy, weights, *held)


def ffn_gradient(acts, h, dy, blocks):
    count, width = h.shape
    units = acts.shape[2]
    feat = width // blocks

    def kernel(left, h_ref, dy_ref, out):
        def store(right):
            result = dot_tn(left[0], right).astype(BF)
            for k in range(PLANE):
                out[0, k, 0] = result[k * (units // PLANE) : (k + 1) * (units // PLANE)]

        part = pl.program_id(1)

        @pl.when(part < 2)
        def _():
            store(h_ref[...])

        @pl.when(part == 2)
        def _():
            store(dy_ref[...])

    right = pl.BlockSpec((count, feat), lambda k, part: (0, k))
    out = pl.pallas_call(
        kernel,
        grid=(blocks, 3),
        in_specs=[pl.BlockSpec((1, count, units), lambda k, part: (part, 0, 0)), right, right],
        out_specs=pl.BlockSpec(
            (1, PLANE, 1, units // PLANE, feat), lambda k, part: (k, 0, part, 0, 0)
        ),
        out_shape=jax.ShapeDtypeStruct((blocks, PLANE, 3, units // PLANE, feat), BF),
        compiler_params=params(),
        cost_estimate=pl.CostEstimate(
            flops=6 * count * width * units, bytes_accessed=24 << 20, transcendentals=0
        ),
        name="ffn_gradient",
    )(acts, h, dy)
    return out.reshape(-1, feat)


def shards(
    tokens,
    out_grad,
    doc_lengths,
    norm_attn,
    w_qdown,
    norm_query,
    w_qup,
    w_key,
    w_value,
    w_out,
    norm_ffn,
    w_gate,
    w_up,
    w_down,
):
    rows, rings = lax.axis_size("rows"), lax.axis_size("ring")
    devices = rows * rings * PLANE
    row = lax.axis_index("rows")
    ring = lax.axis_index("ring")
    plane = lax.axis_index("py") * 2 + lax.axis_index("px")
    spot = (row, ring, plane)
    own_tokens = tokens[0]
    count_local, width = own_tokens.shape
    group = count_local * PLANE
    row_length = group * rings

    latent_width = w_qdown.shape[1] // PLANE
    kv_width = 2 * HD // PLANE
    kv_w = jnp.concatenate([w_key, w_value], axis=1)
    down_w = jnp.concatenate(
        [
            piece
            for i in range(PLANE)
            for piece in (
                w_qdown[:, i * latent_width : (i + 1) * latent_width],
                kv_w[:, i * kv_width : (i + 1) * kv_width],
            )
        ],
        axis=1,
    )
    part_a, part_q = norm_attn.shape[0], norm_query.shape[0]
    gains = jnp.concatenate([norm_attn, norm_query, norm_ffn])
    gain_count = gains.shape[0]
    lanes = latent_width + kv_width
    gains = jnp.tile(jnp.pad(gains, (0, lanes - gain_count)), PLANE)
    gains = jnp.pad(gains[None], ((0, EXTRA - 1), (0, 0)))
    block_rows = down_w.shape[0]
    hidden_axes = ("rows", "py", "px")
    down_w = column_swap(jnp.concatenate([down_w, gains]), plane)
    ffn_w = jnp.concatenate([jnp.transpose(w_gate), jnp.transpose(w_up), w_down])
    token_blocks = plane_spread(own_tokens)
    ffn_w = lax.all_gather(ffn_w, hidden_axes, axis=0, tiled=True)
    down_ring = ring_spread(down_w, "ring")
    other_w = jnp.concatenate([w_qup, jnp.transpose(w_out)])
    other_w = column_swap(other_w, plane)
    other_w = other_w.reshape(PLANE, -1, other_w.shape[1])
    up_rows = w_qup.shape[0]
    up_query = other_w[:, :up_rows].reshape(-1, other_w.shape[2])
    out_proj = other_w[:, up_rows:].reshape(-1, other_w.shape[2])
    up_query, *down_ring = tie(up_query, *down_ring)
    down_fin, gains = rows_place(down_ring, row, ring, block_rows)
    up_ring = ring_gather(up_query, "ring")
    out_proj, *up_ring = tie(out_proj, *up_ring)
    out_proj = rows_place(ring_gather(out_proj, "ring"), row, ring)
    upstream = out_grad[0]
    ring_upstream = upstream
    ring_upstream, ffn_w = tie(upstream, ffn_w)
    ring_upstream = lax.all_gather(ring_upstream, "ring", axis=0, tiled=True)
    down_w = down_fin.reshape(-1, lanes)
    gains = gains[:, 0, :gain_count].astype(F32)
    gain_attn = gains[:, :part_a].reshape(-1)
    gain_query = gains[:, part_a : part_a + part_q].reshape(-1)
    gain_ffn = gains[:, part_a + part_q :].reshape(-1)

    key_positions = jnp.arange(row_length, dtype=jnp.int32)
    key_relative = doc_layout(doc_lengths[0], key_positions)[1]
    key_cos, key_sin = rope_tables(key_relative, HD // 2)
    scal = jnp.concatenate([jnp.stack([plane, ring * group]), doc_lengths[0]]).astype(jnp.int32)

    group_tokens = plane_place(token_blocks, plane).astype(F32)
    normed = rms_norm(group_tokens, gain_attn).astype(BF)
    projected = mm(normed, down_w).astype(BF)

    up_query = rows_place(up_ring, row, ring)
    key_value = ring_spread(projected[:, latent_width:], "ring")
    latent = plane_spread(projected[:, :latent_width])
    key_value = ring_place(key_value, ring)
    key_value, *latent = tie(key_value, *latent)
    latent = jnp.stack(latent)
    latent = jnp.concatenate([pick(latent, plane ^ i) for i in range(PLANE)], axis=1).astype(F32)
    latent_normed = rms_norm(latent, gain_query).astype(BF)
    query_raw = mm(latent_normed, up_query)

    key_value = plane_spread(key_value)
    query_raw, out_proj = tie(query_raw, out_proj)
    attended, queries, log_total, all_keys, all_values = attend(
        scal, query_raw, key_value, key_cos, key_sin
    )
    branch = mm_nt(attended, out_proj)
    branch = plane_sum([block_of(branch, plane ^ k, count_local) for k in range(PLANE)])
    middle = own_tokens.astype(F32) + branch

    normed2_f, pull_ffn_norm = jax.vjp(rms_norm, middle, gain_ffn)
    normed_ffn = normed2_f.astype(BF)
    chunk = 2
    chunks = rings // chunk
    held = []
    grad_parts, out_parts = [], []
    ring_normed = [normed_ffn]
    for k in range(1, rings):
        last = ring_normed[-1]
        if k > 1 and k % chunk == chunk - 1:
            last, *held = tie(last, *held)
        ring_normed.append(shift(last, "ring"))
        if k % chunk != chunk - 1:
            continue
        some = slice(k - chunk + 1, k + 1)
        slots = (ring - jnp.arange(k - chunk + 1, k + 1)) % rings
        results = feed_forward(
            k // chunk, chunks, slots, ring_normed[some], ring_upstream, ffn_w, held
        )
        held = results[:3]
        grad_parts += results[3 : 3 + chunk]
        out_parts += results[3 + chunk :]
    grad_normed_ffn = ring_steps(grad_parts, 1, rings - 2)
    ffn_grad, grad_normed_ffn = tie(ffn_gradient(*held, rows), grad_normed_ffn)
    ffn_grad = lax.psum_scatter(ffn_grad, hidden_axes, scatter_dimension=0, tiled=True)
    grad_normed_ffn = ring_steps(grad_parts, rings - 1, rings - 1, grad_normed_ffn)
    grad_normed_ffn, *out_parts = tie(grad_normed_ffn, *out_parts)
    out_total = ring_steps(out_parts, 1, rings - 2)
    output = ring_steps(out_parts, rings - 1, rings - 1, out_total)

    upstream_f = upstream.astype(F32)
    grad_middle_norm, grad_gain_ffn = pull_ffn_norm(grad_normed_ffn)
    grad_middle = upstream_f + grad_middle_norm

    branch_grad = grad_middle.astype(BF)
    branch_blocks = plane_spread(branch_grad)
    branch_grad = plane_place(branch_blocks, plane)
    grad_attended = mm(branch_grad, out_proj).astype(BF)
    grad_query_raw, kv_parts = attend_back(
        scal,
        queries,
        all_keys,
        all_values,
        log_total,
        attended,
        grad_attended,
        key_cos,
        key_sin,
        out_total,
    )
    grad_out_w = over_rows(row_blocks(branch_grad, attended, spot))
    grad_out_w, output = tie(grad_out_w, output)
    output = middle + output
    grad_up_query = over_rows(row_blocks(latent_normed, grad_query_raw, spot))
    both = [g.reshape(rings * PLANE, -1, g.shape[1]) for g in (grad_up_query, grad_out_w)]
    wide_parts = jnp.concatenate(both, axis=1).reshape(-1, grad_out_w.shape[1])
    wide_parts = ring_parts(wide_parts, spot)
    wide_grad = ring_steps(wide_parts, 1, 1)
    grad_latent_normed = mm_nt(grad_query_raw, up_query)
    kv_grad = plane_sum([kv_parts[k] for k in range(PLANE)]).astype(BF)
    kv_grad, grad_latent_normed = tie(kv_grad, grad_latent_normed)
    kv_grad, wide_grad = tie(kv_grad, wide_grad)
    kv_grad = ring_steps(
        [block_of(kv_grad, (ring - k) % rings, group) for k in range(rings)], 1, rings - 1
    )
    wide_grad = ring_steps(wide_parts, 2, rings - 1, wide_grad).astype(BF)
    grad_latent_normed = plane_sum(
        [block_of(grad_latent_normed, plane ^ k, count_local) for k in range(PLANE)]
    )
    own_latent = block_of(latent, plane, count_local)
    pull_latent = jax.vjp(rms_norm, own_latent, gain_query)[1]
    grad_latent, grad_gain_query = pull_latent(grad_latent_normed)
    grad_latent = grad_latent.astype(BF)
    grad_latent = plane_swap(
        [block_of(grad_latent, plane ^ k, latent_width, 1) for k in range(PLANE)]
    )
    grad_latent = place([(g, plane ^ k) for k, g in enumerate(grad_latent)], PLANE)
    grad_projected = jnp.concatenate([grad_latent, kv_grad.astype(BF)], axis=1)
    grad_projected, wide_grad = tie(grad_projected, wide_grad)
    grad_normed = mm_nt(grad_projected, down_w)
    pull_attn_norm = jax.vjp(rms_norm, own_tokens.astype(F32), gain_attn)[1]
    scale = lax.rsqrt(jnp.mean(group_tokens * group_tokens, axis=-1, keepdims=True) + epsilon)
    grad_gain_attn = jnp.sum(grad_normed * group_tokens * scale, axis=0)
    gain_grads = jnp.concatenate(
        [g.reshape(devices, -1) for g in (grad_gain_attn, grad_gain_query, grad_gain_ffn)], axis=1
    )
    gain_grads = jnp.pad(gain_grads[:, None], ((0, 0), (0, EXTRA - 1), (0, lanes - gain_count)))
    gain_grads = gain_grads.reshape(rows, rings * PLANE, EXTRA, lanes)
    grad_down = over_rows(row_blocks(normed, grad_projected, spot, gain_grads))
    down_parts = ring_parts(grad_down, spot)
    ffn_grad = ffn_grad.astype(F32).reshape(3, -1, ffn_grad.shape[1])
    gate_grad, up_grad, down_grad = jnp.transpose(ffn_grad[0]), jnp.transpose(ffn_grad[1]), ffn_grad[2]
    grad_down = ring_steps(down_parts, 1, 1)
    grad_down, grad_normed = tie(grad_down, grad_normed)
    grad_down = ring_steps(down_parts, 2, rings - 1, grad_down)
    grad_down = grad_down.astype(BF)
    grad_up_query, grad_out_w = over_plane(wide_grad, spot, up_rows)
    grad_up_query = jnp.concatenate(list(grad_up_query), axis=1).astype(F32)
    grad_out_w = jnp.transpose(jnp.concatenate(list(grad_out_w), axis=1).astype(F32))
    grad_normed = plane_sum(
        [block_of(grad_normed, plane ^ k, count_local) for k in range(PLANE)]
    )
    grad_input = grad_middle + pull_attn_norm(grad_normed)[0]
    size = grad_down.shape[0] // PLANE
    grad_down = plane_swap([block_of(grad_down, plane ^ k, size) for k in range(PLANE)])
    grad_gains = sum(g[block_rows, :gain_count].astype(F32) for g in grad_down)
    grad_down = jnp.stack([g[:block_rows] for g in grad_down])
    grad_down = [pick(grad_down, plane ^ i).astype(F32) for i in range(PLANE)]
    grad_down_query = jnp.concatenate([p[:, :latent_width] for p in grad_down], axis=1)
    grad_kv_w = jnp.concatenate([p[:, latent_width:] for p in grad_down], axis=1)

    return (
        output.astype(BF)[None],
        grad_input.astype(BF)[None],
        grad_gains[:part_a],
        grad_down_query,
        grad_gains[part_a : part_a + part_q],
        grad_up_query,
        grad_kv_w[:, :HD],
        grad_kv_w[:, HD:],
        grad_out_w,
        grad_gains[part_a + part_q :],
        gate_grad,
        up_grad,
        down_grad,
    )


def solution(mesh):
    rows = mesh.shape["rows"]
    chips = mesh.shape["seq"]
    inner = Mesh(
        np.asarray(mesh.devices).reshape(rows, chips // PLANE, 2, 2), ("rows", "ring", "py", "px")
    )
    seq = ("ring", "py", "px")
    every = ("rows",) + seq
    placed = (
        P("rows", seq, None),
        P("rows", seq, None),
        P("rows", None),
        P(every),
        P(every, None),
        P(every),
        P(every, None),
        P(every, None),
        P(every, None),
        P(None, every),
        P(every),
        P("rows", seq),
        P("rows", seq),
        P(seq, "rows"),
    )
    return jax.shard_map(
        shards,
        mesh=inner,
        in_specs=placed,
        out_specs=(
            P("rows", seq, None),
            P("rows", seq, None),
            P(every),
            P(every, None),
            P(every),
            P(every, None),
            P(every, None),
            P(every, None),
            P(None, every),
            P(every),
            P("rows", seq),
            P("rows", seq),
            P(seq, "rows"),
        ),
        check_vma=False,
    )
```

```python
import jax
import jax.numpy as jnp
import numpy as np
from jax import lax
from jax.experimental import pallas as pl
from jax.experimental.pallas import tpu as pltpu
from jax.sharding import Mesh, PartitionSpec as P

HEADS = 16
HD = 256
PLANE = 4
EXTRA = 16

masked = -1e30
epsilon = 1e-05
BF = jnp.bfloat16
F32 = jnp.float32


def rms_norm(values, gain_vec):
    return (
        values * lax.rsqrt(jnp.mean(values * values, axis=-1, keepdims=True) + epsilon) * gain_vec
    )


def rope_tables(relative, half_dim):
    frequency = 1.0 / 10000.0 ** (jnp.arange(half_dim, dtype=F32) / half_dim)
    angles = relative.astype(F32)[..., None] * frequency
    return (jnp.cos(angles), jnp.sin(angles))


def doc_layout(lengths, positions):
    doc_ends = jnp.cumsum(lengths)
    passed = positions[:, None] >= doc_ends[None, :]
    segment = jnp.sum(passed.astype(jnp.int32), axis=1)
    doc_start = jnp.sum(jnp.where(passed, lengths[None, :], 0), axis=1)
    return (segment, positions - doc_start)


def mm(left, right):
    return jnp.dot(left, right, preferred_element_type=F32)


def mm_nt(left, right):
    return jnp.einsum("ik,jk->ij", left, right, preferred_element_type=F32)


def mm_tn(left, right):
    return jnp.einsum("ki,kj->ij", left, right, preferred_element_type=F32)


def shift(value, axis, by=1):
    count = lax.axis_size(axis)
    return lax.ppermute(value, axis, [(i, (i + by) % count) for i in range(count)])


def ring_gather(value, axis):
    pieces = [value]
    for _ in range(lax.axis_size(axis) - 1):
        pieces.append(shift(pieces[-1], axis))
    return pieces


def ring_spread(value, axis):
    return [value] + [shift(value, axis, k) for k in range(1, lax.axis_size(axis))]


def flip(value, by):
    if by == 3:
        return lax.ppermute(value, ("py", "px"), [(i, i ^ 3) for i in range(PLANE)])
    return lax.ppermute(value, "px" if by == 1 else "py", [(0, 1), (1, 0)])


def halves(value, axis=0):
    half = value.shape[axis] // 2
    return (
        lax.slice_in_dim(value, 0, half, axis=axis),
        lax.slice_in_dim(value, half, 2 * half, axis=axis),
    )


def plane_spread(value):
    return [value] + [flip(value, k) for k in range(1, PLANE)]


def plane_sum(parts):
    got = [flip(parts[k].astype(BF), k) for k in range(1, PLANE)]
    return sum((g.astype(F32) for g in got), parts[0].astype(F32))


def plane_swap(parts):
    return [parts[0]] + [flip(parts[k], k) for k in range(1, PLANE)]


def pick(stacked, index):
    return lax.dynamic_index_in_dim(stacked, index, 0, keepdims=False)


def place(items, count, unit=None, split=None):
    unit = unit or items[0][0].shape[0]
    columns = items[0][0].shape[1]
    pieces = [v.reshape(-1, unit, columns) for v, _ in items]
    number = len(pieces)
    cuts = [(0, unit)] if split is None else [(0, split), (split, unit)]

    def kernel(slots, *refs):
        outs, sems = refs[number:-1], refs[-1]
        copies = []
        for i in range(number):
            span = pl.ds(slots[i], pieces[i].shape[0])
            for j, (start, stop) in enumerate(cuts):
                source = refs[i] if split is None else refs[i].at[:, pl.ds(start, stop - start)]
                copies.append(pltpu.make_async_copy(source, outs[j].at[span], sems.at[i, j]))
        for copy in copies:
            copy.start()
        for copy in copies:
            copy.wait()

    shapes = [(count, stop - start, columns) for start, stop in cuts]
    outs = pl.pallas_call(
        kernel,
        grid_spec=pltpu.PrefetchScalarGridSpec(
            num_scalar_prefetch=1,
            grid=(1,),
            in_specs=[pl.BlockSpec(memory_space=pl.ANY)] * number,
            out_specs=[pl.BlockSpec(shape, lambda i, s: (0, 0, 0)) for shape in shapes],
            scratch_shapes=[pltpu.SemaphoreType.DMA((number, len(cuts)))],
        ),
        out_shape=[jax.ShapeDtypeStruct(shape, pieces[0].dtype) for shape in shapes],
        compiler_params=params(),
        cost_estimate=pl.CostEstimate(
            flops=0, bytes_accessed=4 * count * unit * columns, transcendentals=0
        ),
        name="place",
    )(jnp.stack([jnp.asarray(slot, jnp.int32) for _, slot in items]), *pieces)
    if split is None:
        return outs[0].reshape(-1, columns)
    return outs


def plane_place(blocks, index):
    return place([(p, index ^ k) for k, p in enumerate(blocks)], PLANE)


def ring_place(pieces, index):
    count = len(pieces)
    return place([(p, (index - k) % count) for k, p in enumerate(pieces)], count)


def block_of(value, index, size, axis=0):
    return lax.dynamic_slice_in_dim(value, index * size, size, axis)


def column_swap(weight, index):
    size = weight.shape[1] // PLANE
    parts = [block_of(weight, index ^ k, size, 1) for k in range(PLANE)]
    return place([(p, index ^ k) for k, p in enumerate(plane_swap(parts))], PLANE)


def rows_place(pieces, row, ring, split=None):
    rings, rows = len(pieces), lax.axis_size("rows")
    unit = pieces[0].shape[0] // PLANE
    own = ring_place(pieces, ring)
    items = [
        (got, (row - j) % rows * rings * PLANE) for j, got in enumerate(ring_spread(own, "rows"))
    ]
    return place(items, rings * rows * PLANE, unit, split)


def row_blocks(left, right, spot, extra=None):
    row, rows = spot[0], lax.axis_size("rows")
    size = left.shape[1] // rows

    def block(k):
        index = (row - k) % rows
        result = mm_tn(block_of(left, index, size, 1), right)
        if extra is not None:
            more = pick(extra, index)
            result = result.reshape(more.shape[0], -1, result.shape[1])
            result = jnp.concatenate([result, more], axis=1).reshape(-1, result.shape[2])
        return result

    return block


def over_rows(block):
    rows = lax.axis_size("rows")
    total = block(1).astype(BF) if rows > 1 else block(0)
    for k in range(2, rows + 1):
        total = shift(total, "rows").astype(F32) + block(k % rows)
        total = total.astype(BF)
    return total


def ring_parts(total, spot):
    ring, rings = spot[1], lax.axis_size("ring")
    size = total.shape[0] // rings
    return [block_of(total, (ring - k) % rings, size) for k in range(rings)]


def over_plane(total, spot, split):
    plane = spot[2]
    size = total.shape[0] // PLANE
    got = plane_swap([block_of(total, plane ^ k, size) for k in range(PLANE)])
    return place([(g, plane ^ k) for k, g in enumerate(got)], PLANE, None, split)


def ring_steps(parts, first, last, total=None):
    count = len(parts)
    total = parts[1] if total is None else total
    for k in range(first + 1, last + 2):
        total = shift(total, "ring").astype(F32) + parts[k % count].astype(F32)
        if k < count:
            total = total.astype(BF)
    return total


def tie(value, *deps):
    return lax.optimization_barrier((value,) + deps)


def params():
    return pltpu.CompilerParams(vmem_limit_bytes=56 * 1024 * 1024)


def dot_nn(left, right):
    return lax.dot_general(left, right, (((1,), (0,)), ((), ())), preferred_element_type=F32)


def dot_nt(left, right):
    return lax.dot_general(left, right, (((1,), (1,)), ((), ())), preferred_element_type=F32)


def dot_tn(left, right):
    return lax.dot_general(left, right, (((0,), (0,)), ((), ())), preferred_element_type=F32)


QB = 256
KB = 512
HALF = HD // 2


def query_bounds(scal, ndoc, block):
    first = scal[1] + block * QB
    positions = first + lax.broadcasted_iota(jnp.int32, (QB, 1), 0)
    starts = jnp.zeros((QB, 1), jnp.int32)
    low_start, end = 0, 0
    for n in range(ndoc):
        end = end + scal[2 + n]
        starts = jnp.where(positions >= end, end, starts)
        low_start = jnp.where(first >= end, end, low_start)
    return positions, starts, lax.div(low_start, KB), lax.div(first + QB - 1, KB) + 1


def attend_kernel(ndoc, scal, q_raw, p0, p1, p2, p3, cos, sin, att, q_out, lse, keys, values):
    block = pl.program_id(0)
    heads = q_raw.shape[1] // HD

    @pl.when(block == 0)
    def _():
        plane = scal[0]
        for i in range(PLANE):
            dest = keys if i < 2 else values
            side = slice((i % 2) * HALF, (i % 2 + 1) * HALF)
            for j, piece in enumerate((p0, p1, p2, p3)):

                @pl.when(plane == (i ^ j))
                def _(dest=dest, side=side, piece=piece):
                    dest[:, side] = piece[...]

        front, back = keys[:, :HALF].astype(F32), keys[:, HALF:].astype(F32)
        keys[:, :HALF] = (front * cos[...] - back * sin[...]).astype(BF)
        keys[:, HALF:] = (back * cos[...] + front * sin[...]).astype(BF)

    rows = pl.ds(pl.multiple_of(scal[1] + block * QB, QB), QB)
    q_cos, q_sin = cos[rows, :], sin[rows, :]
    for h in range(heads):
        front = q_raw[:, h * HD : h * HD + HALF]
        back = q_raw[:, h * HD + HALF : (h + 1) * HD]
        query = jnp.concatenate(
            [front * q_cos - back * q_sin, back * q_cos + front * q_sin], axis=1
        ).astype(BF)
        q_out[:, h * HD : (h + 1) * HD] = query * jnp.asarray(HD**-0.5, BF)
    positions, starts, low, high = query_bounds(scal, ndoc, block)

    def step(kb, carry):
        span = pl.ds(pl.multiple_of(kb * KB, KB), KB)
        where = kb * KB + lax.broadcasted_iota(jnp.int32, (QB, KB), 1)
        allowed = (where <= positions) & (where >= starts)
        key, value = keys[span, :], values[span, :]
        result = []
        for h in range(heads):
            peak, total, mixed = carry[h]
            scores = dot_nt(q_out[:, h * HD : (h + 1) * HD], key)
            scores = jnp.where(allowed, scores, masked)
            new_peak = jnp.maximum(peak, jnp.max(scores, axis=1, keepdims=True))
            weights = jnp.exp(scores - new_peak)
            keep = jnp.exp(peak - new_peak)
            total = total * keep + jnp.sum(weights, axis=1, keepdims=True)
            mixed = mixed * keep + dot_nn(weights.astype(BF), value)
            result.append((new_peak, total, mixed))
        return tuple(result)

    first = (jnp.full((QB, 1), -3e38, F32), jnp.zeros((QB, 1), F32), jnp.zeros((QB, HD), F32))
    done = lax.fori_loop(low, high, step, (first,) * heads)
    for h, (peak, total, mixed) in enumerate(done):
        att[:, h * HD : (h + 1) * HD] = (mixed / total).astype(BF)
        lse[:, h * 128 : (h + 1) * 128] = jnp.broadcast_to(peak + jnp.log(total), (QB, 128))


def attend(scal, query_raw, pieces, cos, sin):
    group, wide = query_raw.shape
    length = cos.shape[0]
    heads = wide // HD
    whole = pl.BlockSpec((length, HALF), lambda i, s: (0, 0))
    token = pl.BlockSpec((QB, wide), lambda i, s: (i, 0))
    return pl.pallas_call(
        lambda *refs: attend_kernel(scal.shape[0] - 2, *refs),
        grid_spec=pltpu.PrefetchScalarGridSpec(
            num_scalar_prefetch=1,
            grid=(group // QB,),
            in_specs=[token] + [whole] * 6,
            out_specs=[
                token,
                token,
                pl.BlockSpec((QB, heads * 128), lambda i, s: (i, 0)),
                pl.BlockSpec((length, HD), lambda i, s: (0, 0)),
                pl.BlockSpec((length, HD), lambda i, s: (0, 0)),
            ],
        ),
        out_shape=[
            jax.ShapeDtypeStruct((group, wide), BF),
            jax.ShapeDtypeStruct((group, wide), BF),
            jax.ShapeDtypeStruct((group, heads * 128), F32),
            jax.ShapeDtypeStruct((length, HD), BF),
            jax.ShapeDtypeStruct((length, HD), BF),
        ],
        compiler_params=params(),
        cost_estimate=pl.CostEstimate(
            flops=4 * group * wide * length, bytes_accessed=8 << 20, transcendentals=0
        ),
        name="attend",
    )(scal, query_raw, *pieces, cos, sin)


def attend_back_kernel(
    ndoc, scal, query, keys, values, lse, att, d_att, cos, sin, dep, d_raw, parts, d_keys, d_values
):
    block = pl.program_id(0)
    heads = query.shape[1] // HD

    @pl.when(block == 0)
    def _():
        d_keys[...] = jnp.zeros_like(d_keys)
        d_values[...] = jnp.zeros_like(d_values)

    positions, starts, low, high = query_bounds(scal, ndoc, block)
    spans = [slice(h * HD, (h + 1) * HD) for h in range(heads)]
    shared = [
        jnp.sum(d_att[:, s].astype(F32) * att[:, s].astype(F32), axis=1, keepdims=True)
        for s in spans
    ]

    def step(kb, d_queries):
        span = pl.ds(pl.multiple_of(kb * KB, KB), KB)
        key, value = keys[span, :], values[span, :]
        where = kb * KB + lax.broadcasted_iota(jnp.int32, (QB, KB), 1)
        allowed = (where <= positions) & (where >= starts)
        result = []
        d_key, d_value = d_keys[span, :], d_values[span, :]
        for h in range(heads):
            scores = dot_nt(query[:, spans[h]], key)
            scores = jnp.where(allowed, scores, masked)
            probs = jnp.exp(scores - lse[:, h * 128 : h * 128 + 1])
            d_probs = dot_nt(d_att[:, spans[h]], value)
            d_scores = (probs * (d_probs - shared[h])).astype(BF)
            d_key = d_key + dot_tn(d_scores, query[:, spans[h]])
            d_value = d_value + dot_tn(probs.astype(BF), d_att[:, spans[h]])
            result.append(d_queries[h] + dot_nn(d_scores, key))
        d_keys[span, :] = d_key
        d_values[span, :] = d_value
        return tuple(result)

    done = lax.fori_loop(low, high, step, (jnp.zeros((QB, HD), F32),) * heads)
    rows = pl.ds(pl.multiple_of(scal[1] + block * QB, QB), QB)
    q_cos, q_sin = cos[rows, :], sin[rows, :]
    for h, d_query in enumerate(done):
        d_query = d_query * HD**-0.5
        front, back = d_query[:, :HALF], d_query[:, HALF:]
        d_raw[:, h * HD : h * HD + HALF] = (front * q_cos + back * q_sin).astype(BF)
        d_raw[:, h * HD + HALF : (h + 1) * HD] = (back * q_cos - front * q_sin).astype(BF)

    @pl.when(block == pl.num_programs(0) - 1)
    def _():
        plane = scal[0]
        front, back = d_keys[:, :HALF], d_keys[:, HALF:]
        parts[plane] = (front * cos[...] + back * sin[...]).astype(BF)
        parts[plane ^ 1] = (back * cos[...] - front * sin[...]).astype(BF)
        parts[plane ^ 2] = d_values[:, :HALF].astype(BF)
        parts[plane ^ 3] = d_values[:, HALF:].astype(BF)


def attend_back(scal, query, keys, values, lse, att, d_att, cos, sin, dep):
    group, wide = query.shape
    length = cos.shape[0]
    heads = wide // HD
    token = pl.BlockSpec((QB, wide), lambda i, s: (i, 0))
    table = pl.BlockSpec((length, HALF), lambda i, s: (0, 0))
    whole = pl.BlockSpec((length, HD), lambda i, s: (0, 0))
    return pl.pallas_call(
        lambda *refs: attend_back_kernel(scal.shape[0] - 2, *refs),
        grid_spec=pltpu.PrefetchScalarGridSpec(
            num_scalar_prefetch=1,
            grid=(group // QB,),
            in_specs=[token, whole, whole, pl.BlockSpec((QB, heads * 128), lambda i, s: (i, 0))]
            + [token, token, table, table, pl.BlockSpec(memory_space=pl.ANY)],
            out_specs=[token, pl.BlockSpec((PLANE, length, HALF), lambda i, s: (0, 0, 0))],
            scratch_shapes=[pltpu.VMEM((length, HD), F32), pltpu.VMEM((length, HD), F32)],
        ),
        out_shape=[
            jax.ShapeDtypeStruct((group, wide), BF),
            jax.ShapeDtypeStruct((PLANE, length, HALF), BF),
        ],
        compiler_params=params(),
        cost_estimate=pl.CostEstimate(
            flops=10 * group * wide * length, bytes_accessed=12 << 20, transcendentals=0
        ),
        name="attend_back",
    )(scal, query, keys, values, lse, att, d_att, cos, sin, dep)


def ffn_kernel(chunk, count, blocks, slots, *refs):
    h_refs, dy_ref, w_ref, refs = refs[:count], refs[count], refs[count + 1], refs[count + 2 :]
    if chunk:
        refs = refs[3:]
    acts, h_all, dy_all = refs[:3]
    d_h, out = refs[3 : 3 + count], refs[3 + count : 3 + 2 * count]
    gate_up, down, sems, dy_sems = refs[3 + 2 * count :]
    units = down.shape[1]
    own = units // PLANE
    rows = h_refs[0].shape[0]
    copies = []
    for block in range(blocks):
        for k in range(PLANE):
            at = block * PLANE + k
            for part in range(3):
                source = w_ref.at[pl.ds((3 * at + part) * own, own)]
                if part < 2:
                    dest = gate_up.at[block, pl.ds(part * units + k * own, own)]
                else:
                    dest = down.at[block, pl.ds(k * own, own)]
                copies.append((part, pltpu.make_async_copy(source, dest, sems.at[at, part])))
    for k in range(count):
        source = dy_ref.at[pl.ds(pl.multiple_of(slots[k] * rows, rows), rows)]
        dest = dy_all.at[pl.ds(k * rows, rows)]
        copies.insert(0, (2, pltpu.make_async_copy(source, dest, dy_sems.at[k])))
    for part in range(3):
        for kind, copy in copies:
            if kind == part:
                copy.start()
    for k in range(count):
        h_all[k * rows : (k + 1) * rows, :] = h_refs[k][...]
    feat = h_all.shape[1] // blocks

    def cols(ref, k):
        return ref[:, k * feat : (k + 1) * feat]

    def wait(part):
        for kind, copy in copies:
            if kind == part:
                copy.wait()

    wait(0)
    gate = sum(dot_nt(cols(h_all, k), gate_up[k, :units, :]) for k in range(blocks))
    wait(1)
    up = sum(dot_nt(cols(h_all, k), gate_up[k, units:, :]) for k in range(blocks))
    sig = 1.0 / (1.0 + jnp.exp(-gate))
    silu = gate * sig
    hid = (silu * up).astype(BF)
    acts[2] = hid
    wait(2)
    d_hidden = sum(dot_nt(cols(dy_all, k), down[k]) for k in range(blocks))
    d_gate = (d_hidden * up * (sig + silu * (1.0 - sig))).astype(BF)
    d_up = (d_hidden * silu).astype(BF)
    acts[0] = d_gate
    acts[1] = d_up
    for k in range(blocks):
        span = slice(k * feat, (k + 1) * feat)
        grad = dot_nn(d_gate, gate_up[k, :units, :]) + dot_nn(d_up, gate_up[k, units:, :])
        result = dot_nn(hid, down[k])
        for j in range(count):
            d_h[j][:, span] = grad[j * rows : (j + 1) * rows].astype(BF)
            out[j][:, span] = result[j * rows : (j + 1) * rows].astype(BF)


def feed_forward(chunk, chunks, slots, h, dy, weights, held):
    count = len(h)
    rows, width = h[0].shape
    feat = weights.shape[1]
    blocks = width // feat
    units = weights.shape[0] // blocks // 3
    total = rows * count
    whole = pl.BlockSpec((rows, width), lambda i, s: (0, 0))
    anywhere = pl.BlockSpec(memory_space=pl.ANY)
    return pl.pallas_call(
        lambda *refs: ffn_kernel(chunk, count, blocks, *refs),
        grid_spec=pltpu.PrefetchScalarGridSpec(
            num_scalar_prefetch=1,
            grid=(1,),
            in_specs=[whole] * count + [anywhere] * (2 + len(held)),
            out_specs=[pl.BlockSpec((3, total, units), lambda i, s: (0, chunk, 0))]
            + [pl.BlockSpec((total, width), lambda i, s: (chunk, 0))] * 2
            + [whole] * (2 * count),
            scratch_shapes=[
                pltpu.VMEM((blocks, 2 * units, feat), BF),
                pltpu.VMEM((blocks, units, feat), BF),
                pltpu.SemaphoreType.DMA((blocks * PLANE, 3)),
                pltpu.SemaphoreType.DMA((count,)),
            ],
        ),
        out_shape=[jax.ShapeDtypeStruct((3, total * chunks, units), BF)]
        + [jax.ShapeDtypeStruct((total * chunks, width), BF)] * 2
        + [jax.ShapeDtypeStruct((rows, width), BF)] * (2 * count),
        input_output_aliases={3 + count + i: i for i in range(len(held))},
        compiler_params=params(),
        cost_estimate=pl.CostEstimate(
            flops=12 * total * width * units, bytes_accessed=24 << 20, transcendentals=0
        ),
        name="feed_forward",
    )(slots, *h, dy, weights, *held)


def ffn_gradient(acts, h, dy, blocks):
    count, width = h.shape
    units = acts.shape[2]
    feat = width // blocks

    def kernel(left, h_ref, dy_ref, out):
        def store(right):
            result = dot_tn(left[0], right).astype(BF)
            for k in range(PLANE):
                out[0, k, 0] = result[k * (units // PLANE) : (k + 1) * (units // PLANE)]

        part = pl.program_id(1)

        @pl.when(part < 2)
        def _():
            store(h_ref[...])

        @pl.when(part == 2)
        def _():
            store(dy_ref[...])

    right = pl.BlockSpec((count, feat), lambda k, part: (0, k))
    out = pl.pallas_call(
        kernel,
        grid=(blocks, 3),
        in_specs=[pl.BlockSpec((1, count, units), lambda k, part: (part, 0, 0)), right, right],
        out_specs=pl.BlockSpec(
            (1, PLANE, 1, units // PLANE, feat), lambda k, part: (k, 0, part, 0, 0)
        ),
        out_shape=jax.ShapeDtypeStruct((blocks, PLANE, 3, units // PLANE, feat), BF),
        compiler_params=params(),
        cost_estimate=pl.CostEstimate(
            flops=6 * count * width * units, bytes_accessed=24 << 20, transcendentals=0
        ),
        name="ffn_gradient",
    )(acts, h, dy)
    return out.reshape(-1, feat)


def shards(
    tokens,
    out_grad,
    doc_lengths,
    norm_attn,
    w_qdown,
    norm_query,
    w_qup,
    w_key,
    w_value,
    w_out,
    norm_ffn,
    w_gate,
    w_up,
    w_down,
):
    rows, rings = lax.axis_size("rows"), lax.axis_size("ring")
    devices = rows * rings * PLANE
    row = lax.axis_index("rows")
    ring = lax.axis_index("ring")
    plane = lax.axis_index("py") * 2 + lax.axis_index("px")
    spot = (row, ring, plane)
    own_tokens = tokens[0]
    count_local, width = own_tokens.shape
    group = count_local * PLANE
    row_length = group * rings

    latent_width = w_qdown.shape[1] // PLANE
    kv_width = 2 * HD // PLANE
    kv_w = jnp.concatenate([w_key, w_value], axis=1)
    down_w = jnp.concatenate(
        [
            piece
            for i in range(PLANE)
            for piece in (
                w_qdown[:, i * latent_width : (i + 1) * latent_width],
                kv_w[:, i * kv_width : (i + 1) * kv_width],
            )
        ],
        axis=1,
    )
    part_a, part_q = norm_attn.shape[0], norm_query.shape[0]
    gains = jnp.concatenate([norm_attn, norm_query, norm_ffn])
    gain_count = gains.shape[0]
    lanes = latent_width + kv_width
    gains = jnp.tile(jnp.pad(gains, (0, lanes - gain_count)), PLANE)
    gains = jnp.pad(gains[None], ((0, EXTRA - 1), (0, 0)))
    block_rows = down_w.shape[0]
    hidden_axes = ("rows", "py", "px")
    down_w = column_swap(jnp.concatenate([down_w, gains]), plane)
    ffn_w = jnp.concatenate([jnp.transpose(w_gate), jnp.transpose(w_up), w_down])
    token_blocks = plane_spread(own_tokens)
    ffn_w = lax.all_gather(ffn_w, hidden_axes, axis=0, tiled=True)
    down_ring = ring_spread(down_w, "ring")
    other_w = jnp.concatenate([w_qup, jnp.transpose(w_out)])
    other_w = column_swap(other_w, plane)
    other_w = other_w.reshape(PLANE, -1, other_w.shape[1])
    up_rows = w_qup.shape[0]
    up_query = other_w[:, :up_rows].reshape(-1, other_w.shape[2])
    out_proj = other_w[:, up_rows:].reshape(-1, other_w.shape[2])
    up_query, *down_ring = tie(up_query, *down_ring)
    down_fin, gains = rows_place(down_ring, row, ring, block_rows)
    up_ring = ring_gather(up_query, "ring")
    out_proj, *up_ring = tie(out_proj, *up_ring)
    out_proj = rows_place(ring_gather(out_proj, "ring"), row, ring)
    upstream = out_grad[0]
    ring_upstream = upstream
    ring_upstream, ffn_w = tie(upstream, ffn_w)
    ring_upstream = lax.all_gather(ring_upstream, "ring", axis=0, tiled=True)
    down_w = down_fin.reshape(-1, lanes)
    gains = gains[:, 0, :gain_count].astype(F32)
    gain_attn = gains[:, :part_a].reshape(-1)
    gain_query = gains[:, part_a : part_a + part_q].reshape(-1)
    gain_ffn = gains[:, part_a + part_q :].reshape(-1)

    key_positions = jnp.arange(row_length, dtype=jnp.int32)
    key_relative = doc_layout(doc_lengths[0], key_positions)[1]
    key_cos, key_sin = rope_tables(key_relative, HD // 2)
    scal = jnp.concatenate([jnp.stack([plane, ring * group]), doc_lengths[0]]).astype(jnp.int32)

    group_tokens = plane_place(token_blocks, plane).astype(F32)
    normed = rms_norm(group_tokens, gain_attn).astype(BF)
    projected = mm(normed, down_w).astype(BF)

    up_query = rows_place(up_ring, row, ring)
    key_value = ring_spread(projected[:, latent_width:], "ring")
    latent = plane_spread(projected[:, :latent_width])
    key_value = ring_place(key_value, ring)
    key_value, *latent = tie(key_value, *latent)
    latent = jnp.stack(latent)
    latent = jnp.concatenate([pick(latent, plane ^ i) for i in range(PLANE)], axis=1).astype(F32)
    latent_normed = rms_norm(latent, gain_query).astype(BF)
    query_raw = mm(latent_normed, up_query)

    key_value = plane_spread(key_value)
    query_raw, out_proj = tie(query_raw, out_proj)
    attended, queries, log_total, all_keys, all_values = attend(
        scal, query_raw, key_value, key_cos, key_sin
    )
    branch = mm_nt(attended, out_proj)
    branch = plane_sum([block_of(branch, plane ^ k, count_local) for k in range(PLANE)])
    middle = own_tokens.astype(F32) + branch

    normed2_f, pull_ffn_norm = jax.vjp(rms_norm, middle, gain_ffn)
    normed_ffn = normed2_f.astype(BF)
    chunk = 2
    chunks = rings // chunk
    held = []
    grad_parts, out_parts = [], []
    ring_normed = [normed_ffn]
    for k in range(1, rings):
        last = ring_normed[-1]
        if k > 1 and k % chunk == chunk - 1:
            last, *held = tie(last, *held)
        ring_normed.append(shift(last, "ring"))
        if k % chunk != chunk - 1:
            continue
        some = slice(k - chunk + 1, k + 1)
        slots = (ring - jnp.arange(k - chunk + 1, k + 1)) % rings
        results = feed_forward(
            k // chunk, chunks, slots, ring_normed[some], ring_upstream, ffn_w, held
        )
        held = results[:3]
        grad_parts += results[3 : 3 + chunk]
        out_parts += results[3 + chunk :]
    grad_normed_ffn = ring_steps(grad_parts, 1, rings - 2)
    ffn_grad, grad_normed_ffn = tie(ffn_gradient(*held, rows), grad_normed_ffn)
    ffn_grad = lax.psum_scatter(ffn_grad, hidden_axes, scatter_dimension=0, tiled=True)
    grad_normed_ffn = ring_steps(grad_parts, rings - 1, rings - 1, grad_normed_ffn)
    grad_normed_ffn, *out_parts = tie(grad_normed_ffn, *out_parts)
    out_total = ring_steps(out_parts, 1, rings - 2)
    output = ring_steps(out_parts, rings - 1, rings - 1, out_total)

    upstream_f = upstream.astype(F32)
    grad_middle_norm, grad_gain_ffn = pull_ffn_norm(grad_normed_ffn)
    grad_middle = upstream_f + grad_middle_norm

    branch_grad = grad_middle.astype(BF)
    branch_blocks = plane_spread(branch_grad)
    branch_grad = plane_place(branch_blocks, plane)
    grad_attended = mm(branch_grad, out_proj).astype(BF)
    grad_query_raw, kv_parts = attend_back(
        scal,
        queries,
        all_keys,
        all_values,
        log_total,
        attended,
        grad_attended,
        key_cos,
        key_sin,
        out_total,
    )
    grad_out_w = over_rows(row_blocks(branch_grad, attended, spot))
    grad_out_w, output = tie(grad_out_w, output)
    output = middle + output
    grad_up_query = over_rows(row_blocks(latent_normed, grad_query_raw, spot))
    both = [g.reshape(rings * PLANE, -1, g.shape[1]) for g in (grad_up_query, grad_out_w)]
    wide_parts = jnp.concatenate(both, axis=1).reshape(-1, grad_out_w.shape[1])
    wide_parts = ring_parts(wide_parts, spot)
    wide_grad = ring_steps(wide_parts, 1, 1)
    grad_latent_normed = mm_nt(grad_query_raw, up_query)
    kv_grad = plane_sum([kv_parts[k] for k in range(PLANE)]).astype(BF)
    kv_grad, grad_latent_normed = tie(kv_grad, grad_latent_normed)
    kv_grad, wide_grad = tie(kv_grad, wide_grad)
    kv_grad = ring_steps(
        [block_of(kv_grad, (ring - k) % rings, group) for k in range(rings)], 1, rings - 1
    )
    wide_grad = ring_steps(wide_parts, 2, rings - 1, wide_grad).astype(BF)
    grad_latent_normed = plane_sum(
        [block_of(grad_latent_normed, plane ^ k, count_local) for k in range(PLANE)]
    )
    own_latent = block_of(latent, plane, count_local)
    pull_latent = jax.vjp(rms_norm, own_latent, gain_query)[1]
    grad_latent, grad_gain_query = pull_latent(grad_latent_normed)
    grad_latent = grad_latent.astype(BF)
    grad_latent = plane_swap(
        [block_of(grad_latent, plane ^ k, latent_width, 1) for k in range(PLANE)]
    )
    grad_latent = place([(g, plane ^ k) for k, g in enumerate(grad_latent)], PLANE)
    grad_projected = jnp.concatenate([grad_latent, kv_grad.astype(BF)], axis=1)
    grad_projected, wide_grad = tie(grad_projected, wide_grad)
    grad_normed = mm_nt(grad_projected, down_w)
    pull_attn_norm = jax.vjp(rms_norm, own_tokens.astype(F32), gain_attn)[1]
    scale = lax.rsqrt(jnp.mean(group_tokens * group_tokens, axis=-1, keepdims=True) + epsilon)
    grad_gain_attn = jnp.sum(grad_normed * group_tokens * scale, axis=0)
    gain_grads = jnp.concatenate(
        [g.reshape(devices, -1) for g in (grad_gain_attn, grad_gain_query, grad_gain_ffn)], axis=1
    )
    gain_grads = jnp.pad(gain_grads[:, None], ((0, 0), (0, EXTRA - 1), (0, lanes - gain_count)))
    gain_grads = gain_grads.reshape(rows, rings * PLANE, EXTRA, lanes)
    grad_down = over_rows(row_blocks(normed, grad_projected, spot, gain_grads))
    down_parts = ring_parts(grad_down, spot)
    ffn_grad = ffn_grad.astype(F32).reshape(3, -1, ffn_grad.shape[1])
    gate_grad, up_grad, down_grad = jnp.transpose(ffn_grad[0]), jnp.transpose(ffn_grad[1]), ffn_grad[2]
    grad_down = ring_steps(down_parts, 1, 1)
    grad_down, grad_normed = tie(grad_down, grad_normed)
    grad_down = ring_steps(down_parts, 2, rings - 1, grad_down)
    grad_down = grad_down.astype(BF)
    grad_up_query, grad_out_w = over_plane(wide_grad, spot, up_rows)
    grad_up_query = jnp.concatenate(list(grad_up_query), axis=1).astype(F32)
    grad_out_w = jnp.transpose(jnp.concatenate(list(grad_out_w), axis=1).astype(F32))
    grad_normed = plane_sum(
        [block_of(grad_normed, plane ^ k, count_local) for k in range(PLANE)]
    )
    grad_input = grad_middle + pull_attn_norm(grad_normed)[0]
    size = grad_down.shape[0] // PLANE
    grad_down = plane_swap([block_of(grad_down, plane ^ k, size) for k in range(PLANE)])
    grad_gains = sum(g[block_rows, :gain_count].astype(F32) for g in grad_down)
    grad_down = jnp.stack([g[:block_rows] for g in grad_down])
    grad_down = [pick(grad_down, plane ^ i).astype(F32) for i in range(PLANE)]
    grad_down_query = jnp.concatenate([p[:, :latent_width] for p in grad_down], axis=1)
    grad_kv_w = jnp.concatenate([p[:, latent_width:] for p in grad_down], axis=1)

    return (
        output.astype(BF)[None],
        grad_input.astype(BF)[None],
        grad_gains[:part_a],
        grad_down_query,
        grad_gains[part_a : part_a + part_q],
        grad_up_query,
        grad_kv_w[:, :HD],
        grad_kv_w[:, HD:],
        grad_out_w,
        grad_gains[part_a + part_q :],
        gate_grad,
        up_grad,
        down_grad,
    )


def solution(mesh):
    rows = mesh.shape["rows"]
    chips = mesh.shape["seq"]
    inner = Mesh(
        np.asarray(mesh.devices).reshape(rows, chips // PLANE, 2, 2), ("rows", "ring", "py", "px")
    )
    seq = ("ring", "py", "px")
    every = ("rows",) + seq
    placed = (
        P("rows", seq, None),
        P("rows", seq, None),
        P("rows", None),
        P(every),
        P(every, None),
        P(every),
        P(every, None),
        P(every, None),
        P(every, None),
        P(None, every),
        P(every),
        P("rows", seq),
        P("rows", seq),
        P(seq, "rows"),
    )
    return jax.shard_map(
        shards,
        mesh=inner,
        in_specs=placed,
        out_specs=(
            P("rows", seq, None),
            P("rows", seq, None),
            P(every),
            P(every, None),
            P(every),
            P(every, None),
            P(every, None),
            P(every, None),
            P(None, every),
            P(every),
            P("rows", seq),
            P("rows", seq),
            P(seq, "rows"),
        ),
        check_vma=False,
    )
```

```python
import jax
import jax.numpy as jnp
import numpy as np
from jax import lax
from jax.experimental import pallas as pl
from jax.experimental.pallas import tpu as pltpu
from jax.sharding import Mesh, PartitionSpec as P

HEADS = 16
HD = 256
PLANE = 4
EXTRA = 16

masked = -1e30
epsilon = 1e-05
BF = jnp.bfloat16
F32 = jnp.float32


def rms_norm(values, gain_vec):
    return (
        values * lax.rsqrt(jnp.mean(values * values, axis=-1, keepdims=True) + epsilon) * gain_vec
    )


def rope_tables(relative, half_dim):
    frequency = 1.0 / 10000.0 ** (jnp.arange(half_dim, dtype=F32) / half_dim)
    angles = relative.astype(F32)[..., None] * frequency
    return (jnp.cos(angles), jnp.sin(angles))


def doc_layout(lengths, positions):
    doc_ends = jnp.cumsum(lengths)
    passed = positions[:, None] >= doc_ends[None, :]
    segment = jnp.sum(passed.astype(jnp.int32), axis=1)
    doc_start = jnp.sum(jnp.where(passed, lengths[None, :], 0), axis=1)
    return (segment, positions - doc_start)


def mm(left, right):
    return jnp.dot(left, right, preferred_element_type=F32)


def mm_nt(left, right):
    return jnp.einsum("ik,jk->ij", left, right, preferred_element_type=F32)


def mm_tn(left, right):
    return jnp.einsum("ki,kj->ij", left, right, preferred_element_type=F32)


def shift(value, axis, by=1):
    count = lax.axis_size(axis)
    return lax.ppermute(value, axis, [(i, (i + by) % count) for i in range(count)])


def ring_gather(value, axis):
    pieces = [value]
    for _ in range(lax.axis_size(axis) - 1):
        pieces.append(shift(pieces[-1], axis))
    return pieces


def ring_spread(value, axis):
    return [value] + [shift(value, axis, k) for k in range(1, lax.axis_size(axis))]


def flip(value, by):
    if by == 3:
        return lax.ppermute(value, ("py", "px"), [(i, i ^ 3) for i in range(PLANE)])
    return lax.ppermute(value, "px" if by == 1 else "py", [(0, 1), (1, 0)])


def halves(value, axis=0):
    half = value.shape[axis] // 2
    return (
        lax.slice_in_dim(value, 0, half, axis=axis),
        lax.slice_in_dim(value, half, 2 * half, axis=axis),
    )


def plane_spread(value):
    return [value] + [flip(value, k) for k in range(1, PLANE)]


def plane_sum(parts):
    got = [flip(parts[k].astype(BF), k) for k in range(1, PLANE)]
    return sum((g.astype(F32) for g in got), parts[0].astype(F32))


def plane_swap(parts):
    return [parts[0]] + [flip(parts[k], k) for k in range(1, PLANE)]


def pick(stacked, index):
    return lax.dynamic_index_in_dim(stacked, index, 0, keepdims=False)


def place(items, count, unit=None, split=None):
    unit = unit or items[0][0].shape[0]
    columns = items[0][0].shape[1]
    pieces = [v.reshape(-1, unit, columns) for v, _ in items]
    number = len(pieces)
    cuts = [(0, unit)] if split is None else [(0, split), (split, unit)]

    def kernel(slots, *refs):
        outs, sems = refs[number:-1], refs[-1]
        copies = []
        for i in range(number):
            span = pl.ds(slots[i], pieces[i].shape[0])
            for j, (start, stop) in enumerate(cuts):
                source = refs[i] if split is None else refs[i].at[:, pl.ds(start, stop - start)]
                copies.append(pltpu.make_async_copy(source, outs[j].at[span], sems.at[i, j]))
        for copy in copies:
            copy.start()
        for copy in copies:
            copy.wait()

    shapes = [(count, stop - start, columns) for start, stop in cuts]
    outs = pl.pallas_call(
        kernel,
        grid_spec=pltpu.PrefetchScalarGridSpec(
            num_scalar_prefetch=1,
            grid=(1,),
            in_specs=[pl.BlockSpec(memory_space=pl.ANY)] * number,
            out_specs=[pl.BlockSpec(shape, lambda i, s: (0, 0, 0)) for shape in shapes],
            scratch_shapes=[pltpu.SemaphoreType.DMA((number, len(cuts)))],
        ),
        out_shape=[jax.ShapeDtypeStruct(shape, pieces[0].dtype) for shape in shapes],
        compiler_params=params(),
        cost_estimate=pl.CostEstimate(
            flops=0, bytes_accessed=4 * count * unit * columns, transcendentals=0
        ),
        name="place",
    )(jnp.stack([jnp.asarray(slot, jnp.int32) for _, slot in items]), *pieces)
    if split is None:
        return outs[0].reshape(-1, columns)
    return outs


def plane_place(blocks, index):
    return place([(p, index ^ k) for k, p in enumerate(blocks)], PLANE)


def ring_place(pieces, index):
    count = len(pieces)
    return place([(p, (index - k) % count) for k, p in enumerate(pieces)], count)


def block_of(value, index, size, axis=0):
    return lax.dynamic_slice_in_dim(value, index * size, size, axis)


def column_swap(weight, index):
    size = weight.shape[1] // PLANE
    parts = [block_of(weight, index ^ k, size, 1) for k in range(PLANE)]
    return place([(p, index ^ k) for k, p in enumerate(plane_swap(parts))], PLANE)


def rows_place(pieces, row, ring, split=None):
    rings, rows = len(pieces), lax.axis_size("rows")
    unit = pieces[0].shape[0] // PLANE
    own = ring_place(pieces, ring)
    items = [
        (got, (row - j) % rows * rings * PLANE) for j, got in enumerate(ring_spread(own, "rows"))
    ]
    return place(items, rings * rows * PLANE, unit, split)


def row_blocks(left, right, spot, extra=None):
    row, rows = spot[0], lax.axis_size("rows")
    size = left.shape[1] // rows

    def block(k):
        index = (row - k) % rows
        result = mm_tn(block_of(left, index, size, 1), right)
        if extra is not None:
            more = pick(extra, index)
            result = result.reshape(more.shape[0], -1, result.shape[1])
            result = jnp.concatenate([result, more], axis=1).reshape(-1, result.shape[2])
        return result

    return block


def over_rows(block):
    rows = lax.axis_size("rows")
    total = block(1).astype(BF) if rows > 1 else block(0)
    for k in range(2, rows + 1):
        total = shift(total, "rows").astype(F32) + block(k % rows)
        total = total.astype(BF)
    return total


def ring_parts(total, spot):
    ring, rings = spot[1], lax.axis_size("ring")
    size = total.shape[0] // rings
    return [block_of(total, (ring - k) % rings, size) for k in range(rings)]


def over_plane(total, spot, split):
    plane = spot[2]
    size = total.shape[0] // PLANE
    got = plane_swap([block_of(total, plane ^ k, size) for k in range(PLANE)])
    return place([(g, plane ^ k) for k, g in enumerate(got)], PLANE, None, split)


def ring_steps(parts, first, last, total=None):
    count = len(parts)
    total = parts[1] if total is None else total
    for k in range(first + 1, last + 2):
        total = shift(total, "ring").astype(F32) + parts[k % count].astype(F32)
        if k < count:
            total = total.astype(BF)
    return total


def tie(value, *deps):
    return lax.optimization_barrier((value,) + deps)


def params():
    return pltpu.CompilerParams(vmem_limit_bytes=56 * 1024 * 1024)


def dot_nn(left, right):
    return lax.dot_general(left, right, (((1,), (0,)), ((), ())), preferred_element_type=F32)


def dot_nt(left, right):
    return lax.dot_general(left, right, (((1,), (1,)), ((), ())), preferred_element_type=F32)


def dot_tn(left, right):
    return lax.dot_general(left, right, (((0,), (0,)), ((), ())), preferred_element_type=F32)


QB = 256
KB = 512
HALF = HD // 2


def query_bounds(scal, ndoc, block):
    first = scal[1] + block * QB
    positions = first + lax.broadcasted_iota(jnp.int32, (QB, 1), 0)
    starts = jnp.zeros((QB, 1), jnp.int32)
    low_start, end = 0, 0
    for n in range(ndoc):
        end = end + scal[2 + n]
        starts = jnp.where(positions >= end, end, starts)
        low_start = jnp.where(first >= end, end, low_start)
    return positions, starts, lax.div(low_start, KB), lax.div(first + QB - 1, KB) + 1


def attend_kernel(ndoc, scal, q_raw, p0, p1, p2, p3, cos, sin, att, q_out, lse, keys, values):
    block = pl.program_id(0)
    heads = q_raw.shape[1] // HD

    @pl.when(block == 0)
    def _():
        plane = scal[0]
        for i in range(PLANE):
            dest = keys if i < 2 else values
            side = slice((i % 2) * HALF, (i % 2 + 1) * HALF)
            for j, piece in enumerate((p0, p1, p2, p3)):

                @pl.when(plane == (i ^ j))
                def _(dest=dest, side=side, piece=piece):
                    dest[:, side] = piece[...]

        front, back = keys[:, :HALF].astype(F32), keys[:, HALF:].astype(F32)
        keys[:, :HALF] = (front * cos[...] - back * sin[...]).astype(BF)
        keys[:, HALF:] = (back * cos[...] + front * sin[...]).astype(BF)

    rows = pl.ds(pl.multiple_of(scal[1] + block * QB, QB), QB)
    q_cos, q_sin = cos[rows, :], sin[rows, :]
    for h in range(heads):
        front = q_raw[:, h * HD : h * HD + HALF]
        back = q_raw[:, h * HD + HALF : (h + 1) * HD]
        query = jnp.concatenate(
            [front * q_cos - back * q_sin, back * q_cos + front * q_sin], axis=1
        ).astype(BF)
        q_out[:, h * HD : (h + 1) * HD] = query * jnp.asarray(HD**-0.5, BF)
    positions, starts, low, high = query_bounds(scal, ndoc, block)

    def step(kb, carry):
        span = pl.ds(pl.multiple_of(kb * KB, KB), KB)
        where = kb * KB + lax.broadcasted_iota(jnp.int32, (QB, KB), 1)
        allowed = (where <= positions) & (where >= starts)
        key, value = keys[span, :], values[span, :]
        result = []
        for h in range(heads):
            peak, total, mixed = carry[h]
            scores = dot_nt(q_out[:, h * HD : (h + 1) * HD], key)
            scores = jnp.where(allowed, scores, masked)
            new_peak = jnp.maximum(peak, jnp.max(scores, axis=1, keepdims=True))
            weights = jnp.exp(scores - new_peak)
            keep = jnp.exp(peak - new_peak)
            total = total * keep + jnp.sum(weights, axis=1, keepdims=True)
            mixed = mixed * keep + dot_nn(weights.astype(BF), value)
            result.append((new_peak, total, mixed))
        return tuple(result)

    first = (jnp.full((QB, 1), -3e38, F32), jnp.zeros((QB, 1), F32), jnp.zeros((QB, HD), F32))
    done = lax.fori_loop(low, high, step, (first,) * heads)
    for h, (peak, total, mixed) in enumerate(done):
        att[:, h * HD : (h + 1) * HD] = (mixed / total).astype(BF)
        lse[:, h * 128 : (h + 1) * 128] = jnp.broadcast_to(peak + jnp.log(total), (QB, 128))


def attend(scal, query_raw, pieces, cos, sin):
    group, wide = query_raw.shape
    length = cos.shape[0]
    heads = wide // HD
    whole = pl.BlockSpec((length, HALF), lambda i, s: (0, 0))
    token = pl.BlockSpec((QB, wide), lambda i, s: (i, 0))
    return pl.pallas_call(
        lambda *refs: attend_kernel(scal.shape[0] - 2, *refs),
        grid_spec=pltpu.PrefetchScalarGridSpec(
            num_scalar_prefetch=1,
            grid=(group // QB,),
            in_specs=[token] + [whole] * 6,
            out_specs=[
                token,
                token,
                pl.BlockSpec((QB, heads * 128), lambda i, s: (i, 0)),
                pl.BlockSpec((length, HD), lambda i, s: (0, 0)),
                pl.BlockSpec((length, HD), lambda i, s: (0, 0)),
            ],
        ),
        out_shape=[
            jax.ShapeDtypeStruct((group, wide), BF),
            jax.ShapeDtypeStruct((group, wide), BF),
            jax.ShapeDtypeStruct((group, heads * 128), F32),
            jax.ShapeDtypeStruct((length, HD), BF),
            jax.ShapeDtypeStruct((length, HD), BF),
        ],
        compiler_params=params(),
        cost_estimate=pl.CostEstimate(
            flops=4 * group * wide * length, bytes_accessed=8 << 20, transcendentals=0
        ),
        name="attend",
    )(scal, query_raw, *pieces, cos, sin)


def attend_back_kernel(
    ndoc, scal, query, keys, values, lse, att, d_att, cos, sin, dep, d_raw, parts, d_keys, d_values
):
    block = pl.program_id(0)
    heads = query.shape[1] // HD

    @pl.when(block == 0)
    def _():
        d_keys[...] = jnp.zeros_like(d_keys)
        d_values[...] = jnp.zeros_like(d_values)

    positions, starts, low, high = query_bounds(scal, ndoc, block)
    spans = [slice(h * HD, (h + 1) * HD) for h in range(heads)]
    shared = [
        jnp.sum(d_att[:, s].astype(F32) * att[:, s].astype(F32), axis=1, keepdims=True)
        for s in spans
    ]

    def step(kb, d_queries):
        span = pl.ds(pl.multiple_of(kb * KB, KB), KB)
        key, value = keys[span, :], values[span, :]
        where = kb * KB + lax.broadcasted_iota(jnp.int32, (QB, KB), 1)
        allowed = (where <= positions) & (where >= starts)
        result = []
        d_key, d_value = d_keys[span, :], d_values[span, :]
        for h in range(heads):
            scores = dot_nt(query[:, spans[h]], key)
            scores = jnp.where(allowed, scores, masked)
            probs = jnp.exp(scores - lse[:, h * 128 : h * 128 + 1])
            d_probs = dot_nt(d_att[:, spans[h]], value)
            d_scores = (probs * (d_probs - shared[h])).astype(BF)
            d_key = d_key + dot_tn(d_scores, query[:, spans[h]])
            d_value = d_value + dot_tn(probs.astype(BF), d_att[:, spans[h]])
            result.append(d_queries[h] + dot_nn(d_scores, key))
        d_keys[span, :] = d_key
        d_values[span, :] = d_value
        return tuple(result)

    done = lax.fori_loop(low, high, step, (jnp.zeros((QB, HD), F32),) * heads)
    rows = pl.ds(pl.multiple_of(scal[1] + block * QB, QB), QB)
    q_cos, q_sin = cos[rows, :], sin[rows, :]
    for h, d_query in enumerate(done):
        d_query = d_query * HD**-0.5
        front, back = d_query[:, :HALF], d_query[:, HALF:]
        d_raw[:, h * HD : h * HD + HALF] = (front * q_cos + back * q_sin).astype(BF)
        d_raw[:, h * HD + HALF : (h + 1) * HD] = (back * q_cos - front * q_sin).astype(BF)

    @pl.when(block == pl.num_programs(0) - 1)
    def _():
        plane = scal[0]
        front, back = d_keys[:, :HALF], d_keys[:, HALF:]
        parts[plane] = (front * cos[...] + back * sin[...]).astype(BF)
        parts[plane ^ 1] = (back * cos[...] - front * sin[...]).astype(BF)
        parts[plane ^ 2] = d_values[:, :HALF].astype(BF)
        parts[plane ^ 3] = d_values[:, HALF:].astype(BF)


def attend_back(scal, query, keys, values, lse, att, d_att, cos, sin, dep):
    group, wide = query.shape
    length = cos.shape[0]
    heads = wide // HD
    token = pl.BlockSpec((QB, wide), lambda i, s: (i, 0))
    table = pl.BlockSpec((length, HALF), lambda i, s: (0, 0))
    whole = pl.BlockSpec((length, HD), lambda i, s: (0, 0))
    return pl.pallas_call(
        lambda *refs: attend_back_kernel(scal.shape[0] - 2, *refs),
        grid_spec=pltpu.PrefetchScalarGridSpec(
            num_scalar_prefetch=1,
            grid=(group // QB,),
            in_specs=[token, whole, whole, pl.BlockSpec((QB, heads * 128), lambda i, s: (i, 0))]
            + [token, token, table, table, pl.BlockSpec(memory_space=pl.ANY)],
            out_specs=[token, pl.BlockSpec((PLANE, length, HALF), lambda i, s: (0, 0, 0))],
            scratch_shapes=[pltpu.VMEM((length, HD), F32), pltpu.VMEM((length, HD), F32)],
        ),
        out_shape=[
            jax.ShapeDtypeStruct((group, wide), BF),
            jax.ShapeDtypeStruct((PLANE, length, HALF), BF),
        ],
        compiler_params=params(),
        cost_estimate=pl.CostEstimate(
            flops=10 * group * wide * length, bytes_accessed=12 << 20, transcendentals=0
        ),
        name="attend_back",
    )(scal, query, keys, values, lse, att, d_att, cos, sin, dep)


def ffn_kernel(chunk, count, blocks, slots, *refs):
    h_refs, dy_ref, w_ref, refs = refs[:count], refs[count], refs[count + 1], refs[count + 2 :]
    if chunk:
        refs = refs[3:]
    acts, h_all, dy_all = refs[:3]
    d_h, out = refs[3 : 3 + count], refs[3 + count : 3 + 2 * count]
    gate_up, down, sems, dy_sems = refs[3 + 2 * count :]
    units = down.shape[1]
    own = units // PLANE
    rows = h_refs[0].shape[0]
    copies = []
    for block in range(blocks):
        for k in range(PLANE):
            at = block * PLANE + k
            for part in range(3):
                source = w_ref.at[pl.ds((3 * at + part) * own, own)]
                if part < 2:
                    dest = gate_up.at[block, pl.ds(part * units + k * own, own)]
                else:
                    dest = down.at[block, pl.ds(k * own, own)]
                copies.append((part, pltpu.make_async_copy(source, dest, sems.at[at, part])))
    for k in range(count):
        source = dy_ref.at[pl.ds(pl.multiple_of(slots[k] * rows, rows), rows)]
        dest = dy_all.at[pl.ds(k * rows, rows)]
        copies.insert(0, (2, pltpu.make_async_copy(source, dest, dy_sems.at[k])))
    for part in range(3):
        for kind, copy in copies:
            if kind == part:
                copy.start()
    for k in range(count):
        h_all[k * rows : (k + 1) * rows, :] = h_refs[k][...]
    feat = h_all.shape[1] // blocks

    def cols(ref, k):
        return ref[:, k * feat : (k + 1) * feat]

    def wait(part):
        for kind, copy in copies:
            if kind == part:
                copy.wait()

    wait(0)
    gate = sum(dot_nt(cols(h_all, k), gate_up[k, :units, :]) for k in range(blocks))
    wait(1)
    up = sum(dot_nt(cols(h_all, k), gate_up[k, units:, :]) for k in range(blocks))
    sig = 1.0 / (1.0 + jnp.exp(-gate))
    silu = gate * sig
    hid = (silu * up).astype(BF)
    acts[2] = hid
    wait(2)
    d_hidden = sum(dot_nt(cols(dy_all, k), down[k]) for k in range(blocks))
    d_gate = (d_hidden * up * (sig + silu * (1.0 - sig))).astype(BF)
    d_up = (d_hidden * silu).astype(BF)
    acts[0] = d_gate
    acts[1] = d_up
    for k in range(blocks):
        span = slice(k * feat, (k + 1) * feat)
        grad = dot_nn(d_gate, gate_up[k, :units, :]) + dot_nn(d_up, gate_up[k, units:, :])
        result = dot_nn(hid, down[k])
        for j in range(count):
            d_h[j][:, span] = grad[j * rows : (j + 1) * rows].astype(BF)
            out[j][:, span] = result[j * rows : (j + 1) * rows].astype(BF)


def feed_forward(chunk, chunks, slots, h, dy, weights, held):
    count = len(h)
    rows, width = h[0].shape
    feat = weights.shape[1]
    blocks = width // feat
    units = weights.shape[0] // blocks // 3
    total = rows * count
    whole = pl.BlockSpec((rows, width), lambda i, s: (0, 0))
    anywhere = pl.BlockSpec(memory_space=pl.ANY)
    return pl.pallas_call(
        lambda *refs: ffn_kernel(chunk, count, blocks, *refs),
        grid_spec=pltpu.PrefetchScalarGridSpec(
            num_scalar_prefetch=1,
            grid=(1,),
            in_specs=[whole] * count + [anywhere] * (2 + len(held)),
            out_specs=[pl.BlockSpec((3, total, units), lambda i, s: (0, chunk, 0))]
            + [pl.BlockSpec((total, width), lambda i, s: (chunk, 0))] * 2
            + [whole] * (2 * count),
            scratch_shapes=[
                pltpu.VMEM((blocks, 2 * units, feat), BF),
                pltpu.VMEM((blocks, units, feat), BF),
                pltpu.SemaphoreType.DMA((blocks * PLANE, 3)),
                pltpu.SemaphoreType.DMA((count,)),
            ],
        ),
        out_shape=[jax.ShapeDtypeStruct((3, total * chunks, units), BF)]
        + [jax.ShapeDtypeStruct((total * chunks, width), BF)] * 2
        + [jax.ShapeDtypeStruct((rows, width), BF)] * (2 * count),
        input_output_aliases={3 + count + i: i for i in range(len(held))},
        compiler_params=params(),
        cost_estimate=pl.CostEstimate(
            flops=12 * total * width * units, bytes_accessed=24 << 20, transcendentals=0
        ),
        name="feed_forward",
    )(slots, *h, dy, weights, *held)


def ffn_gradient(acts, h, dy, blocks):
    count, width = h.shape
    units = acts.shape[2]
    feat = width // blocks

    def kernel(left, h_ref, dy_ref, out):
        def store(right):
            result = dot_tn(left[0], right).astype(BF)
            for k in range(PLANE):
                out[0, k, 0] = result[k * (units // PLANE) : (k + 1) * (units // PLANE)]

        part = pl.program_id(1)

        @pl.when(part < 2)
        def _():
            store(h_ref[...])

        @pl.when(part == 2)
        def _():
            store(dy_ref[...])

    right = pl.BlockSpec((count, feat), lambda k, part: (0, k))
    out = pl.pallas_call(
        kernel,
        grid=(blocks, 3),
        in_specs=[pl.BlockSpec((1, count, units), lambda k, part: (part, 0, 0)), right, right],
        out_specs=pl.BlockSpec(
            (1, PLANE, 1, units // PLANE, feat), lambda k, part: (k, 0, part, 0, 0)
        ),
        out_shape=jax.ShapeDtypeStruct((blocks, PLANE, 3, units // PLANE, feat), BF),
        compiler_params=params(),
        cost_estimate=pl.CostEstimate(
            flops=6 * count * width * units, bytes_accessed=24 << 20, transcendentals=0
        ),
        name="ffn_gradient",
    )(acts, h, dy)
    return out.reshape(-1, feat)


def shards(
    tokens,
    out_grad,
    doc_lengths,
    norm_attn,
    w_qdown,
    norm_query,
    w_qup,
    w_key,
    w_value,
    w_out,
    norm_ffn,
    w_gate,
    w_up,
    w_down,
):
    rows, rings = lax.axis_size("rows"), lax.axis_size("ring")
    devices = rows * rings * PLANE
    row = lax.axis_index("rows")
    ring = lax.axis_index("ring")
    plane = lax.axis_index("py") * 2 + lax.axis_index("px")
    spot = (row, ring, plane)
    own_tokens = tokens[0]
    count_local, width = own_tokens.shape
    group = count_local * PLANE
    row_length = group * rings

    latent_width = w_qdown.shape[1] // PLANE
    kv_width = 2 * HD // PLANE
    kv_w = jnp.concatenate([w_key, w_value], axis=1)
    down_w = jnp.concatenate(
        [
            piece
            for i in range(PLANE)
            for piece in (
                w_qdown[:, i * latent_width : (i + 1) * latent_width],
                kv_w[:, i * kv_width : (i + 1) * kv_width],
            )
        ],
        axis=1,
    )
    part_a, part_q = norm_attn.shape[0], norm_query.shape[0]
    gains = jnp.concatenate([norm_attn, norm_query, norm_ffn])
    gain_count = gains.shape[0]
    lanes = latent_width + kv_width
    gains = jnp.tile(jnp.pad(gains, (0, lanes - gain_count)), PLANE)
    gains = jnp.pad(gains[None], ((0, EXTRA - 1), (0, 0)))
    block_rows = down_w.shape[0]
    hidden_axes = ("rows", "py", "px")
    down_w = column_swap(jnp.concatenate([down_w, gains]), plane)
    ffn_w = jnp.concatenate([jnp.transpose(w_gate), jnp.transpose(w_up), w_down])
    group_tokens = lax.all_gather(own_tokens, ("py", "px"), axis=0, tiled=True)
    down_ring = ring_spread(down_w, "ring")
    ffn_w, group_tokens, *down_ring = tie(ffn_w, group_tokens, *down_ring)
    ffn_w = lax.all_gather(ffn_w, hidden_axes, axis=0, tiled=True)
    other_w = jnp.concatenate([w_qup, jnp.transpose(w_out)])
    other_w = column_swap(other_w, plane)
    other_w = other_w.reshape(PLANE, -1, other_w.shape[1])
    up_rows = w_qup.shape[0]
    up_query = other_w[:, :up_rows].reshape(-1, other_w.shape[2])
    out_proj = other_w[:, up_rows:].reshape(-1, other_w.shape[2])
    up_query, *down_ring = tie(up_query, *down_ring)
    down_fin, gains = rows_place(down_ring, row, ring, block_rows)
    up_ring = ring_gather(up_query, "ring")
    out_proj, *up_ring = tie(out_proj, *up_ring)
    out_proj = rows_place(ring_gather(out_proj, "ring"), row, ring)
    upstream = out_grad[0]
    ring_upstream = upstream
    ring_upstream, ffn_w = tie(upstream, ffn_w)
    ring_upstream = lax.all_gather(ring_upstream, "ring", axis=0, tiled=True)
    down_w = down_fin.reshape(-1, lanes)
    gains = gains[:, 0, :gain_count].astype(F32)
    gain_attn = gains[:, :part_a].reshape(-1)
    gain_query = gains[:, part_a : part_a + part_q].reshape(-1)
    gain_ffn = gains[:, part_a + part_q :].reshape(-1)

    key_positions = jnp.arange(row_length, dtype=jnp.int32)
    key_relative = doc_layout(doc_lengths[0], key_positions)[1]
    key_cos, key_sin = rope_tables(key_relative, HD // 2)
    scal = jnp.concatenate([jnp.stack([plane, ring * group]), doc_lengths[0]]).astype(jnp.int32)

    group_tokens = group_tokens.astype(F32)
    normed = rms_norm(group_tokens, gain_attn).astype(BF)
    projected = mm(normed, down_w).astype(BF)

    up_query = rows_place(up_ring, row, ring)
    key_value = ring_spread(projected[:, latent_width:], "ring")
    latent = plane_spread(projected[:, :latent_width])
    key_value = ring_place(key_value, ring)
    key_value, *latent = tie(key_value, *latent)
    latent = jnp.stack(latent)
    latent = jnp.concatenate([pick(latent, plane ^ i) for i in range(PLANE)], axis=1).astype(F32)
    latent_normed = rms_norm(latent, gain_query).astype(BF)
    query_raw = mm(latent_normed, up_query)

    key_value = plane_spread(key_value)
    query_raw, out_proj = tie(query_raw, out_proj)
    attended, queries, log_total, all_keys, all_values = attend(
        scal, query_raw, key_value, key_cos, key_sin
    )
    branch = mm_nt(attended, out_proj)
    branch = plane_sum([block_of(branch, plane ^ k, count_local) for k in range(PLANE)])
    middle = own_tokens.astype(F32) + branch

    normed2_f, pull_ffn_norm = jax.vjp(rms_norm, middle, gain_ffn)
    normed_ffn = normed2_f.astype(BF)
    chunk = 2
    chunks = rings // chunk
    held = []
    grad_parts, out_parts = [], []
    ring_normed = [normed_ffn]
    for k in range(1, rings):
        last = ring_normed[-1]
        if k > 1 and k % chunk == chunk - 1:
            last, *held = tie(last, *held)
        ring_normed.append(shift(last, "ring"))
        if k % chunk != chunk - 1:
            continue
        some = slice(k - chunk + 1, k + 1)
        slots = (ring - jnp.arange(k - chunk + 1, k + 1)) % rings
        results = feed_forward(
            k // chunk, chunks, slots, ring_normed[some], ring_upstream, ffn_w, held
        )
        held = results[:3]
        grad_parts += results[3 : 3 + chunk]
        out_parts += results[3 + chunk :]
    grad_normed_ffn = ring_steps(grad_parts, 1, rings - 2)
    ffn_grad, grad_normed_ffn = tie(ffn_gradient(*held, rows), grad_normed_ffn)
    ffn_grad = lax.psum_scatter(ffn_grad, hidden_axes, scatter_dimension=0, tiled=True)
    grad_normed_ffn = ring_steps(grad_parts, rings - 1, rings - 1, grad_normed_ffn)
    grad_normed_ffn, *out_parts = tie(grad_normed_ffn, *out_parts)
    out_total = ring_steps(out_parts, 1, rings - 2)
    output = ring_steps(out_parts, rings - 1, rings - 1, out_total)

    upstream_f = upstream.astype(F32)
    grad_middle_norm, grad_gain_ffn = pull_ffn_norm(grad_normed_ffn)
    grad_middle = upstream_f + grad_middle_norm

    branch_grad = grad_middle.astype(BF)
    branch_blocks = plane_spread(branch_grad)
    branch_grad = plane_place(branch_blocks, plane)
    grad_attended = mm(branch_grad, out_proj).astype(BF)
    grad_query_raw, kv_parts = attend_back(
        scal,
        queries,
        all_keys,
        all_values,
        log_total,
        attended,
        grad_attended,
        key_cos,
        key_sin,
        out_total,
    )
    grad_out_w = over_rows(row_blocks(branch_grad, attended, spot))
    grad_out_w, output = tie(grad_out_w, output)
    output = middle + output
    grad_up_query = over_rows(row_blocks(latent_normed, grad_query_raw, spot))
    both = [g.reshape(rings * PLANE, -1, g.shape[1]) for g in (grad_up_query, grad_out_w)]
    wide_parts = jnp.concatenate(both, axis=1).reshape(-1, grad_out_w.shape[1])
    wide_parts = ring_parts(wide_parts, spot)
    wide_grad = ring_steps(wide_parts, 1, 1)
    grad_latent_normed = mm_nt(grad_query_raw, up_query)
    kv_grad = plane_sum([kv_parts[k] for k in range(PLANE)]).astype(BF)
    kv_grad, grad_latent_normed = tie(kv_grad, grad_latent_normed)
    kv_grad, wide_grad = tie(kv_grad, wide_grad)
    kv_grad = ring_steps(
        [block_of(kv_grad, (ring - k) % rings, group) for k in range(rings)], 1, rings - 1
    )
    wide_grad = ring_steps(wide_parts, 2, rings - 1, wide_grad).astype(BF)
    grad_latent_normed = plane_sum(
        [block_of(grad_latent_normed, plane ^ k, count_local) for k in range(PLANE)]
    )
    own_latent = block_of(latent, plane, count_local)
    pull_latent = jax.vjp(rms_norm, own_latent, gain_query)[1]
    grad_latent, grad_gain_query = pull_latent(grad_latent_normed)
    grad_latent = grad_latent.astype(BF)
    grad_latent = plane_swap(
        [block_of(grad_latent, plane ^ k, latent_width, 1) for k in range(PLANE)]
    )
    grad_latent = place([(g, plane ^ k) for k, g in enumerate(grad_latent)], PLANE)
    grad_projected = jnp.concatenate([grad_latent, kv_grad.astype(BF)], axis=1)
    grad_projected, wide_grad = tie(grad_projected, wide_grad)
    grad_normed = mm_nt(grad_projected, down_w)
    pull_attn_norm = jax.vjp(rms_norm, own_tokens.astype(F32), gain_attn)[1]
    scale = lax.rsqrt(jnp.mean(group_tokens * group_tokens, axis=-1, keepdims=True) + epsilon)
    grad_gain_attn = jnp.sum(grad_normed * group_tokens * scale, axis=0)
    gain_grads = jnp.concatenate(
        [g.reshape(devices, -1) for g in (grad_gain_attn, grad_gain_query, grad_gain_ffn)], axis=1
    )
    gain_grads = jnp.pad(gain_grads[:, None], ((0, 0), (0, EXTRA - 1), (0, lanes - gain_count)))
    gain_grads = gain_grads.reshape(rows, rings * PLANE, EXTRA, lanes)
    grad_down = over_rows(row_blocks(normed, grad_projected, spot, gain_grads))
    grad_down, wide_grad = tie(grad_down, wide_grad)
    down_parts = ring_parts(grad_down, spot)
    ffn_grad = ffn_grad.astype(F32).reshape(3, -1, ffn_grad.shape[1])
    gate_grad, up_grad, down_grad = jnp.transpose(ffn_grad[0]), jnp.transpose(ffn_grad[1]), ffn_grad[2]
    grad_down = ring_steps(down_parts, 1, 1)
    grad_down, grad_normed, gate_grad, up_grad, down_grad = tie(
        grad_down, grad_normed, gate_grad, up_grad, down_grad
    )
    grad_down = ring_steps(down_parts, 2, rings - 1, grad_down)
    grad_down = grad_down.astype(BF)
    grad_up_query, grad_out_w = over_plane(wide_grad, spot, up_rows)
    grad_up_query = jnp.concatenate(list(grad_up_query), axis=1).astype(F32)
    grad_out_w = jnp.transpose(jnp.concatenate(list(grad_out_w), axis=1).astype(F32))
    grad_normed = plane_sum(
        [block_of(grad_normed, plane ^ k, count_local) for k in range(PLANE)]
    )
    grad_input = grad_middle + pull_attn_norm(grad_normed)[0]
    size = grad_down.shape[0] // PLANE
    grad_down = plane_swap([block_of(grad_down, plane ^ k, size) for k in range(PLANE)])
    grad_gains = sum(g[block_rows, :gain_count].astype(F32) for g in grad_down)
    grad_down = jnp.stack([g[:block_rows] for g in grad_down])
    grad_down = [pick(grad_down, plane ^ i).astype(F32) for i in range(PLANE)]
    grad_down_query = jnp.concatenate([p[:, :latent_width] for p in grad_down], axis=1)
    grad_kv_w = jnp.concatenate([p[:, latent_width:] for p in grad_down], axis=1)

    return (
        output.astype(BF)[None],
        grad_input.astype(BF)[None],
        grad_gains[:part_a],
        grad_down_query,
        grad_gains[part_a : part_a + part_q],
        grad_up_query,
        grad_kv_w[:, :HD],
        grad_kv_w[:, HD:],
        grad_out_w,
        grad_gains[part_a + part_q :],
        gate_grad,
        up_grad,
        down_grad,
    )


def solution(mesh):
    rows = mesh.shape["rows"]
    chips = mesh.shape["seq"]
    inner = Mesh(
        np.asarray(mesh.devices).reshape(rows, chips // PLANE, 2, 2), ("rows", "ring", "py", "px")
    )
    seq = ("ring", "py", "px")
    every = ("rows",) + seq
    placed = (
        P("rows", seq, None),
        P("rows", seq, None),
        P("rows", None),
        P(every),
        P(every, None),
        P(every),
        P(every, None),
        P(every, None),
        P(every, None),
        P(None, every),
        P(every),
        P("rows", seq),
        P("rows", seq),
        P(seq, "rows"),
    )
    return jax.shard_map(
        shards,
        mesh=inner,
        in_specs=placed,
        out_specs=(
            P("rows", seq, None),
            P("rows", seq, None),
            P(every),
            P(every, None),
            P(every),
            P(every, None),
            P(every, None),
            P(every, None),
            P(None, every),
            P(every),
            P("rows", seq),
            P("rows", seq),
            P(seq, "rows"),
        ),
        check_vma=False,
    )
```
